32 devices in a mesh: dp: 2 (over y), context: 8 (over z, x), tensor: 2 (over core).
Axes of the slice: x: 2, y: 2, z: 4, core: 2. Of those that a mesh axis runs over, the one named last changes fastest.
Arguments:
- tokens: bfloat16 [2, 1024, 2304], P('dp', 'context'), may hold values from -6 to 6
- w_query: bfloat16 [2304, 2048], P(('dp', 'context'), 'tensor'), may hold values from -0.21875 to 0.21875
- w_key: bfloat16 [2304, 1024], P(('dp', 'context'), 'tensor'), may hold values from -0.21875 to 0.21875
- w_value: bfloat16 [2304, 1024], P(('dp', 'context'), 'tensor'), may hold values from -0.125 to 0.125
- w_out: bfloat16 [2304, 2048], P(('dp', 'context'), 'tensor'), may hold values from -0.125 to 0.125
- w_gate: bfloat16 [2304, 9216], P(('dp', 'context'), 'tensor'), may hold values from -0.125 to 0.125
- w_up: bfloat16 [2304, 9216], P(('dp', 'context'), 'tensor'), may hold values from -0.125 to 0.125
- w_down: bfloat16 [2304, 9216], P(('dp', 'context'), 'tensor'), may hold values from -0.0625 to 0.0625
- gain_attn_in: bfloat16 [2304], P(('dp', 'context')), may hold values from 0.5 to 1.5
- gain_attn_out: bfloat16 [2304], P(('dp', 'context')), may hold values from 0.5 to 1.5
- gain_ffw_in: bfloat16 [2304], P(('dp', 'context')), may hold values from 0.5 to 1.5
- gain_ffw_out: bfloat16 [2304], P(('dp', 'context')), may hold values from 0.5 to 1.5
- cotangent: float32 [2, 1024, 2304], P('dp', 'context'), may hold values from -6 to 6
Outputs:
- layer_output: bfloat16 [2, 1024, 2304], P('dp', 'context')
- input_grad: float32 [2, 1024, 2304], P('dp', 'context')
- grad_query: float32 [2304, 2048], P(('dp', 'context'), 'tensor')
- grad_key: float32 [2304, 1024], P(('dp', 'context'), 'tensor')
- grad_value: float32 [2304, 1024], P(('dp', 'context'), 'tensor')
- grad_out: float32 [2304, 2048], P(('dp', 'context'), 'tensor')
- grad_gate: float32 [2304, 9216], P(('dp', 'context'), 'tensor')
- grad_up: float32 [2304, 9216], P(('dp', 'context'), 'tensor')
- grad_down: float32 [2304, 9216], P(('dp', 'context'), 'tensor')
- grad_attn_in: float32 [2304], P(('dp', 'context'))
- grad_attn_out: float32 [2304], P(('dp', 'context'))
- grad_ffw_in: float32 [2304], P(('dp', 'context'))
- grad_ffw_out: float32 [2304], P(('dp', 'context'))
The draws below stay inside these ranges and needn't reach their ends.
All inputs are finite; a program needn't handle non-finite values.
Results may differ from the reference program's by a relative error of at most 0.025.
Values may be sent and summed in bfloat16 or wider, within the bound.
No kernel may reach another device: no remote copies, remote signals or barrier semaphores. Data moves between devices by JAX's collectives and lax.ppermute only.
A program may use at most 576 MiB of HBM per device.

```python
import jax
import jax.numpy as jnp
from jax import lax

D = 2304
FF = 9216
HEADS = 8
KV_HEADS = 4
HEAD_DIM = 256
SEQ = 1024
SEQS = 2


def with_spikes(drawn, own_key, source, target, parts, factor):
    def block_of(position):
        return (jnp.arange(drawn.shape[position]) // (drawn.shape[position] // parts)).reshape((-1,) + (1,) * (drawn.ndim - 1 - position))

    near = jax.random.permutation(own_key, parts)[block_of(target)]
    other_side = (block_of(target) + parts // 2) % parts
    return jnp.where((block_of(source) == near) | (block_of(source) == other_side), factor * drawn, drawn)


def block_scale(key, dims, pieces, least, top_value):
    factor_of = 1.0
    for axis_at, parts in pieces:
        draws = jax.random.uniform(jax.random.fold_in(jax.random.fold_in(key, 6), axis_at), (parts,), jnp.float32, least / len(pieces), top_value / len(pieces))
        factor_of = factor_of * jnp.repeat(jnp.exp(draws), dims[axis_at] // parts).reshape((-1,) + (1,) * (len(dims) - 1 - axis_at))
    return factor_of


def noise(key, dims, deviation, bound, cuts=(), held_as=jnp.bfloat16):
    drawn = jax.random.normal(key, dims, jnp.float32) * deviation
    if len(cuts) > 0:
        drawn = block_scale(key, dims, cuts, -0.22, 0.18) * drawn
    return jnp.clip(drawn, min=-bound, max=bound).astype(held_as)


def gaussian_with(own_key, extent, spread, most, shards, heavy, kind=jnp.bfloat16):
    result = spread * jax.random.normal(own_key, extent, jnp.float32)
    if shards:
        result = result * block_scale(own_key, extent, shards, -0.22, 0.18)
    return jnp.clip(with_spikes(result, jax.random.fold_in(own_key, 3), *heavy), -most, most).astype(kind)


def setup_inputs(seed: int = 0) -> dict:
    key_of = jax.random.split(jax.random.key(seed), 14)
    tokens = noise(key_of[0], (SEQS, SEQ, D), 1.0, 6.0, ((0, 2), (1, 8)))
    w_query = noise(key_of[1], (D, HEADS * HEAD_DIM), (D // 3) ** -0.5, 0.21875, ((0, 16), (1, 2)))
    w_key = noise(key_of[2], (D, KV_HEADS * HEAD_DIM), (D // 3) ** -0.5, 0.21875, ((0, 16), (1, 2)))
    w_value = noise(key_of[3], (D, KV_HEADS * HEAD_DIM), D ** -0.5, 0.125, ((0, 16), (1, 2)))
    w_out = noise(key_of[4], (D, HEADS * HEAD_DIM), (HEADS * HEAD_DIM) ** -0.5, 0.125, ((0, 16), (1, 2)))
    w_gate = noise(key_of[5], (D, FF), D ** -0.5, 0.125, ((0, 16), (1, 2)))
    w_up = noise(key_of[6], (D, FF), D ** -0.5, 0.125, ((0, 16), (1, 2)))
    w_down = noise(key_of[7], (D, FF), FF ** -0.5, 0.0625, ((0, 16), (1, 2)))
    gain_attn_in = jnp.clip(1.0 + 0.1 * jax.random.normal(key_of[8], (D,), jnp.float32), 0.5, 1.5).astype(jnp.bfloat16)
    gain_attn_out = jnp.clip(1.0 + 0.1 * jax.random.normal(key_of[9], (D,), jnp.float32), 0.5, 1.5).astype(jnp.bfloat16)
    gain_ffw_in = jnp.clip(1.0 + 0.1 * jax.random.normal(key_of[10], (D,), jnp.float32), 0.5, 1.5).astype(jnp.bfloat16)
    gain_ffw_out = jnp.clip(1.0 + 0.1 * jax.random.normal(key_of[11], (D,), jnp.float32), 0.5, 1.5).astype(jnp.bfloat16)
    cotangent = gaussian_with(key_of[12], (SEQS, SEQ, D), 1.0, 6.0, ((0, 2), (1, 8)), (1, 2, 8, 2.0), jnp.float32)
    return dict(tokens=tokens, w_query=w_query, w_key=w_key, w_value=w_value, w_out=w_out, w_gate=w_gate, w_up=w_up, w_down=w_down, gain_attn_in=gain_attn_in, gain_attn_out=gain_attn_out, gain_ffw_in=gain_ffw_in, gain_ffw_out=gain_ffw_out, cotangent=cotangent)


epsilon = 1e-06
softcap = 50.0
theta = 10000.0

@jax.custom_vjp
def low(v):
    return lax.optimization_barrier(v.astype(jnp.bfloat16)).astype(jnp.float32)

@jax.custom_vjp
def low_back(v):
    return v

def low_keep(v):
    return (low(v), None)

def low_pass(kept, grad):
    return (grad,)

def back_keep(v):
    return (v, None)

def back_low(kept, grad):
    return (low(grad),)
low.defvjp(low_keep, low_pass)
low_back.defvjp(back_keep, back_low)

def matmul(left_side, right_side):
    return jnp.dot(left_side, right_side, precision=lax.Precision.HIGHEST, preferred_element_type=jnp.float32)

def rms_norm(values, scaling):
    return values * lax.rsqrt(lax.optimization_barrier(jnp.mean(values * values, axis=-1, keepdims=True)) + epsilon) * scaling

def rotate(values, positions, direction):
    half_width = values.shape[-1] // 2
    exponent = jnp.arange(half_width, dtype=jnp.float32) * (-2.0 / values.shape[-1])
    angles = direction * positions.astype(jnp.float32)[:, None] * (theta ** exponent)[None, :]
    cosine = jnp.cos(angles)[:, None, :]
    sine_part = jnp.sin(angles)[:, None, :]
    former = values[..., :half_width]
    latter = values[..., half_width:]
    return jnp.concatenate([former * cosine - latter * sine_part, latter * cosine + former * sine_part], axis=-1)

def attend(queries, key_heads, value_heads):
    length = queries.shape[0]
    block_span = min(length, 1024)
    groups = key_heads.shape[1]
    repeat = queries.shape[1] // groups
    key_places = jnp.arange(length, dtype=jnp.int32)

    def query_block(block_index):
        offset = block_index * block_span
        queried = lax.dynamic_slice_in_dim(queries, offset, block_span, 0).reshape(block_span, groups, repeat, HEAD_DIM)
        scores = low_back(jnp.einsum('tgrd,ngd->grtn', queried, key_heads, precision=lax.Precision.HIGHEST) * HEAD_DIM ** (-0.5))
        capped = softcap * jnp.tanh(scores / softcap)
        allowed = key_places[None, :] <= (offset + jnp.arange(block_span, dtype=jnp.int32))[:, None]
        capped = jnp.where(allowed, capped, -1e+30)
        shifted = jnp.exp(capped - lax.optimization_barrier(jnp.max(capped, axis=-1, keepdims=True)))
        probabilities = low(shifted / lax.optimization_barrier(jnp.sum(shifted, axis=-1, keepdims=True)))
        mixed = jnp.einsum('grtn,ngd->tgrd', probabilities, value_heads, precision=lax.Precision.HIGHEST)
        return mixed.reshape(block_span, groups * repeat * HEAD_DIM)
    blocks = lax.map(jax.checkpoint(query_block), jnp.arange(length // block_span, dtype=jnp.int32))
    return blocks.reshape(length, -1)

def layer_one(inputs, weights):
    w_query, w_key, w_value, w_out, w_gate, w_up, w_down, gain_attn_in, gain_attn_out, gain_ffw_in, gain_ffw_out = weights
    length = inputs.shape[0]
    positions = jnp.arange(length, dtype=jnp.int32)
    normed = low(rms_norm(inputs, gain_attn_in))
    query_raw = low_back(matmul(normed, w_query)).reshape(length, HEADS, HEAD_DIM)
    key_raw = low_back(matmul(normed, w_key)).reshape(length, KV_HEADS, HEAD_DIM)
    value_heads = low(low_back(matmul(normed, w_value))).reshape(length, KV_HEADS, HEAD_DIM)
    queries = low(rotate(query_raw, positions, 1.0))
    key_heads = low(rotate(key_raw, positions, 1.0))
    mixed = low(low_back(attend(queries, key_heads, value_heads)))
    projected = low_back(matmul(mixed, w_out.T))
    middle = inputs + rms_norm(projected, gain_attn_out)
    normed_two = low(rms_norm(middle, gain_ffw_in))
    gate_in = low_back(matmul(normed_two, w_gate))
    upward = low_back(matmul(normed_two, w_up))
    hidden = low(jax.nn.gelu(gate_in, approximate=True) * upward)
    branch = low_back(matmul(hidden, w_down.T))
    return middle + rms_norm(branch, gain_ffw_out)

def reference(tokens, w_query, w_key, w_value, w_out, w_gate, w_up, w_down, gain_attn_in, gain_attn_out, gain_ffw_in, gain_ffw_out, cotangent):
    params = (w_query.astype(jnp.float32), w_key.astype(jnp.float32), w_value.astype(jnp.float32), w_out.astype(jnp.float32), w_gate.astype(jnp.float32), w_up.astype(jnp.float32), w_down.astype(jnp.float32), gain_attn_in.astype(jnp.float32), gain_attn_out.astype(jnp.float32), gain_ffw_in.astype(jnp.float32), gain_ffw_out.astype(jnp.float32))

    def forward(inputs, weights):

        def one_sequence(sequence):
            return layer_one(sequence, weights)
        return lax.map(jax.checkpoint(one_sequence), inputs)
    outcome, pullback = jax.vjp(forward, tokens.astype(jnp.float32), params)
    input_grad, grads = pullback(cotangent.astype(jnp.float32))
    return (outcome.astype(jnp.bfloat16), input_grad, grads[0], grads[1], grads[2], grads[3], grads[4], grads[5], grads[6], grads[7], grads[8], grads[9], grads[10])
```

```python
import jax
import jax.numpy as jnp
from jax import lax
from jax.sharding import PartitionSpec as P

HEAD_DIM = 256
LANES = 128

epsilon = 1e-06
softcap = 50.0
theta = 10000.0
floor_value = -1e30
low = jnp.bfloat16
wide = jnp.float32
chip_axes = ("dp", "context")


def product(left_side, right_side):
    return jnp.dot(left_side, right_side, preferred_element_type=wide)


def product_right_t(left_side, right_side):
    return lax.dot_general(left_side, right_side, (((1,), (1,)), ((), ())), preferred_element_type=wide)


def product_left_t(left_side, right_side):
    return lax.dot_general(left_side, right_side, (((0,), (0,)), ((), ())), preferred_element_type=wide)


def inverse_size(values):
    return lax.rsqrt(jnp.mean(values * values, axis=-1, keepdims=True) + epsilon)


def norm_back(unit, inverse, scaling, upstream):
    inner = upstream * scaling
    return inverse * (inner - unit * jnp.mean(inner * unit, axis=-1, keepdims=True))


def turn(values, cosine, sine_part):
    half_width = values.shape[-1] // 2
    former = values[..., :half_width]
    latter = values[..., half_width:]
    return jnp.concatenate(
        [former * cosine - latter * sine_part, latter * cosine + former * sine_part], axis=-1
    )


def geglu(gate_in, upward):
    return jax.nn.gelu(gate_in, approximate=True) * upward


class Slice:
    def __init__(self):
        self.dp = lax.axis_size("dp")
        self.context = lax.axis_size("context")
        self.ranks = self.context // 2
        self.chips = self.dp * self.context
        self.core = lax.axis_index("tensor")
        self.place = lax.axis_index("context")
        self.rank = self.place // 2
        self.side = self.place % 2
        self.me = lax.axis_index(chip_axes)

    def send(self, block, where):
        pairs = []
        for dp in range(self.dp):
            for rank in range(self.ranks):
                for side in range(2):
                    pairs.append(
                        (self.index(dp, rank, side), self.index(*where(dp, rank, side)))
                    )
        return lax.ppermute(block, chip_axes, pairs)

    def index(self, dp, rank, side):
        return (dp * self.ranks + rank % self.ranks) * 2 + side

    def across(self, block):
        return self.send(block, lambda dp, rank, side: (dp, rank, 1 - side))

    def over(self, block):
        return self.send(block, lambda dp, rank, side: (1 - dp, rank, side))

    def along(self, block, step):
        if step % self.ranks == 0:
            return block
        return self.send(block, lambda dp, rank, side: (dp, rank + step, side))

    def swap(self, block):
        return lax.ppermute(block, "tensor", [(0, 1), (1, 0)])

    def ordered(self, mine, other):
        first = self.core == 0
        return jnp.where(first, mine, other), jnp.where(first, other, mine)

    def exchange(self, pick):
        pieces = [pick(self.me)]
        for turn_by in range(1, self.chips):
            pairs = [(chip, chip ^ turn_by) for chip in range(self.chips)]
            pieces.append(lax.ppermute(pick(self.me ^ turn_by), chip_axes, pairs))
        result = jnp.zeros((self.chips,) + pieces[0].shape, pieces[0].dtype)
        for turn_by, piece in enumerate(pieces):
            result = lax.dynamic_update_index_in_dim(result, piece, self.me ^ turn_by, 0)
        return result

    def gather_plane(self, block, groups):
        moved = {step: self.along(block, step) for step in range(self.ranks)}
        gathered = []
        for group in groups:
            here = jnp.stack([moved[step] for step in group])
            gathered.append(jnp.stack([here, self.across(here)]))
        return gathered

    def gather_all(self, block, groups):
        moved = {step: self.along(block, step) for step in range(self.ranks)}
        cut = block.shape[0] // 2
        gathered = []
        for group in groups:
            here = jnp.stack([moved[step] for step in group])
            beside = self.across(here)
            above = self.over(here)
            corner = jnp.concatenate(
                [self.over(beside[:, :cut]), self.across(above[:, cut:])], axis=1
            )
            gathered.append(jnp.stack([here, beside, above, corner]))
        return gathered

    def scatter_plane(self, parts, groups):
        total = 0.0
        for part, group in zip(parts, groups, strict=True):
            here = part[0].astype(wide)
            if part.shape[0] == 2:
                here = here + self.across(part[1]).astype(wide)
            total = total + self.settle(here, group)
        return total

    def settle(self, here, group):
        total = 0.0
        for at, step in enumerate(group):
            piece = here[at]
            if step:
                piece = self.along(piece.astype(low), -step).astype(wide)
            total = total + piece
        return total

    def scatter_all(self, parts, groups):
        total = 0.0
        for part, group in zip(parts, groups, strict=True):
            cut = part.shape[2] // 2
            upper = part[:, :, :cut]
            lower = part[:, :, cut:]
            upper_two = upper[:2].astype(wide) + self.over(upper[2:]).astype(wide)
            lower_two = lower[0::2].astype(wide) + self.across(lower[1::2]).astype(wide)
            upper_one = upper_two[0] + self.across(upper_two[1].astype(low)).astype(wide)
            lower_one = lower_two[0] + self.over(lower_two[1].astype(low)).astype(wide)
            here = jnp.concatenate([upper_one, lower_one], axis=1)
            total = total + self.settle(here, group)
        return total


def body(
    tokens,
    w_query,
    w_key,
    w_value,
    w_out,
    w_gate,
    w_up,
    w_down,
    gain_attn_in,
    gain_attn_out,
    gain_ffw_in,
    gain_ffw_out,
    cotangent,
):
    net = Slice()
    core, chips = net.core, net.chips
    span = tokens.shape[1]
    width = tokens.shape[2]
    half = span // 2
    rows = w_query.shape[0]
    cut_rows = rows // 2
    heads = 2 * w_query.shape[1] // HEAD_DIM
    kv_heads = 2 * w_key.shape[1] // HEAD_DIM
    repeat = heads // kv_heads
    share = net.context // heads
    score_scale = HEAD_DIM ** (-0.5)
    plane_groups = (tuple(range(net.ranks)),)
    all_groups = (tuple(range(net.ranks)),)

    def own_half(array):
        return lax.dynamic_slice_in_dim(array, core * half, half, 0)

    own_tokens = own_half(tokens[0])
    upstream = own_half(cotangent[0])

    gains = jnp.stack([gain_attn_in, gain_attn_out, gain_ffw_in, gain_ffw_out])
    gains = lax.all_to_all(
        jnp.broadcast_to(gains[None], (chips,) + gains.shape), chip_axes, 0, 0, tiled=True
    )
    gains = jnp.transpose(gains, (1, 0, 2)).reshape(4, width).astype(wide)
    scale_in, scale_mid, scale_pre, scale_out = gains[0], gains[1], gains[2], gains[3]

    packed = jnp.concatenate([w_query, w_key, w_value, w_out], axis=1)
    mine = lax.dynamic_slice_in_dim(packed, core * cut_rows, cut_rows, 0)
    theirs = lax.dynamic_slice_in_dim(packed, (1 - core) * cut_rows, cut_rows, 0)
    first, second = net.ordered(mine, net.swap(theirs))
    edges = (0, w_query.shape[1])
    edges = edges + (edges[1] + w_key.shape[1], edges[1] + 2 * w_key.shape[1])
    edges = edges + (packed.shape[1],)

    def by_head(at):
        both = jnp.concatenate(
            [first[:, edges[at] : edges[at + 1]], second[:, edges[at] : edges[at + 1]]], axis=1
        )
        return jnp.transpose(both.reshape(cut_rows, -1, HEAD_DIM), (1, 0, 2))

    head_sets = jnp.concatenate(
        [
            by_head(0),
            jnp.repeat(by_head(1), repeat, axis=0),
            jnp.repeat(by_head(2), repeat, axis=0),
            by_head(3),
        ],
        axis=2,
    )

    def head_set_of(chip):
        return lax.dynamic_index_in_dim(
            head_sets, (chip % net.context) // share, 0, keepdims=False
        )

    part = net.exchange(head_set_of)
    attn_first, attn_second = net.ordered(part, net.swap(part))
    attn_weights = jnp.stack([attn_first, attn_second], axis=1).reshape(width, 4 * HEAD_DIM)
    w_qkv = attn_weights[:, : 3 * HEAD_DIM]
    w_out_head = attn_weights[:, 3 * HEAD_DIM :]

    units = w_gate.shape[1] // chips
    main = units // LANES * LANES
    rest = units - main
    rest_lanes = -(-3 * rest // LANES) * LANES

    def unit_sets(arrays):
        main_parts = [
            jnp.transpose(a[:, : chips * main].reshape(rows, chips, main), (1, 0, 2)) for a in arrays
        ]
        rest_parts = [
            jnp.transpose(a[:, chips * main :].reshape(rows, chips, rest), (1, 0, 2)) for a in arrays
        ]
        blank = jnp.zeros((chips, rows, rest_lanes - 3 * rest), low)
        return jnp.concatenate(main_parts + rest_parts + [blank], axis=2)

    sets = unit_sets([w_gate, w_up, w_down])
    mine = net.exchange(
        lambda chip: lax.dynamic_index_in_dim(sets, chip, 0, keepdims=False)
    ).reshape(width, -1)
    other = net.swap(mine)

    def units_of(at):
        start = 3 * main + at * rest
        return jnp.concatenate(
            [
                mine[:, at * main : (at + 1) * main],
                other[:, at * main : (at + 1) * main],
                mine[:, start : start + rest],
                other[:, start : start + rest],
            ],
            axis=1,
        )

    gate_units, up_units, down_units = units_of(0), units_of(1), units_of(2)

    if share == 1:
        asked = None
    else:
        asked = tuple(range(0, net.ranks, share // 2))
    own_inputs = own_tokens.astype(wide)
    inputs = jnp.concatenate(
        [g.reshape(-1, width) for g in net.gather_plane(own_tokens, plane_groups)]
    ).astype(wide)
    units_in = inputs * inverse_size(inputs)
    normed_low = (units_in * scale_in).astype(low)
    block_places = jnp.concatenate(
        [
            jnp.stack(
                [
                    jnp.stack([(net.rank - step) % net.ranks * 2 + side for step in group])
                    for side in (net.side, 1 - net.side)
                ]
            ).reshape(-1)
            for group in plane_groups
        ]
    )
    offsets = jnp.arange(half, dtype=jnp.int32)
    places = (block_places[:, None] * span + core * half + offsets[None, :]).reshape(-1)
    other_places = places + (1 - 2 * core) * half
    exponent = jnp.arange(HEAD_DIM // 2, dtype=wide) * (-2.0 / HEAD_DIM)
    angles = places.astype(wide)[:, None] * (theta**exponent)[None, :]
    cosine, sine_part = jnp.cos(angles), jnp.sin(angles)

    def asked_rows(array):
        if asked is None:
            return array
        blocks = array.reshape((2, net.ranks, half) + array.shape[1:])
        return jnp.concatenate([blocks[0, step] for step in asked])

    qkv = product(normed_low, w_qkv)
    queries = asked_rows(turn(qkv[:, :HEAD_DIM], cosine, sine_part).astype(low))
    keys = turn(qkv[:, HEAD_DIM : 2 * HEAD_DIM], cosine, sine_part).astype(low)
    values = qkv[:, 2 * HEAD_DIM :].astype(low)
    own_kv = jnp.concatenate([keys, values], axis=1)
    all_kv = jnp.concatenate([own_kv, net.swap(own_kv)])
    all_keys, all_values = all_kv[:, :HEAD_DIM], all_kv[:, HEAD_DIM:]
    key_places = jnp.concatenate([places, other_places])
    allowed = key_places[None, :] <= asked_rows(places)[:, None]
    scores = product_right_t(queries, all_keys) * score_scale
    bent = jnp.tanh(scores / softcap)
    capped = jnp.where(allowed, softcap * bent, floor_value)
    shifted = jnp.exp(capped - jnp.max(capped, axis=-1, keepdims=True))
    probabilities = shifted / jnp.sum(shifted, axis=-1, keepdims=True)
    probabilities_low = probabilities.astype(low)
    mixed_low = product(probabilities_low, all_values).astype(low)

    def plane_parts(array):
        array = array.astype(low)
        if asked is not None:
            return [array.reshape(1, len(asked), half, width)], (asked,)
        parts, start = [], 0
        for group in plane_groups:
            size = 2 * len(group) * half
            parts.append(array[start : start + size].reshape(2, len(group), half, width))
            start += size
        return parts, plane_groups

    projected = net.scatter_plane(*plane_parts(product_right_t(mixed_low, w_out_head)))

    inverse_mid = inverse_size(projected)
    unit_mid = projected * inverse_mid
    middle = own_inputs + unit_mid * scale_mid
    inverse_pre = inverse_size(middle)
    unit_pre = middle * inverse_pre
    normed_two_low = (unit_pre * scale_pre).astype(low)

    all_two = [g.reshape(-1, width) for g in net.gather_all(normed_two_low, all_groups)]
    gates = [product(rows_two, gate_units) for rows_two in all_two]
    ups = [product(rows_two, up_units) for rows_two in all_two]
    hiddens = [geglu(g, u).astype(low) for g, u in zip(gates, ups, strict=True)]

    def all_part(array, group):
        return array.astype(low).reshape(4, len(group), half, width)

    branch = net.scatter_all(
        [
            all_part(product_right_t(h, down_units), group)
            for h, group in zip(hiddens, all_groups, strict=True)
        ],
        all_groups,
    )
    inverse_out = inverse_size(branch)
    unit_out = branch * inverse_out
    own_output = (middle + unit_out * scale_out).astype(low)

    grad_ffw_out = jnp.sum(upstream * unit_out, axis=0)
    d_branch_low = norm_back(unit_out, inverse_out, scale_out, upstream).astype(low)
    all_branch = [g.reshape(-1, width) for g in net.gather_all(d_branch_low, all_groups)]
    d_gates, d_ups, d_twos = [], [], []
    for d_rows, gate_in, upward, group in zip(all_branch, gates, ups, all_groups, strict=True):
        d_hidden = product(d_rows, down_units)
        _, pull = jax.vjp(geglu, gate_in, upward)
        d_gate, d_up = pull(d_hidden)
        d_gates.append(d_gate.astype(low))
        d_ups.append(d_up.astype(low))
        d_twos.append(
            all_part(
                product_right_t(d_gates[-1], gate_units) + product_right_t(d_ups[-1], up_units),
                group,
            )
        )
    d_normed_two = net.scatter_all(d_twos, all_groups)
    grad_ffw_in = jnp.sum(d_normed_two * unit_pre, axis=0)
    d_middle = upstream + norm_back(unit_pre, inverse_pre, scale_pre, d_normed_two)
    grad_attn_out = jnp.sum(d_middle * unit_mid, axis=0)
    d_projected_low = norm_back(unit_mid, inverse_mid, scale_mid, d_middle).astype(low)

    all_two = jnp.concatenate(all_two)
    all_branch = jnp.concatenate(all_branch)
    unit_grads = [
        product_left_t(all_two, jnp.concatenate(d_gates)),
        product_left_t(all_two, jnp.concatenate(d_ups)),
        product_left_t(all_branch, jnp.concatenate(hiddens)),
    ]

    def side_of(at_other):
        mains = [g[:, at_other * main : (at_other + 1) * main] for g in unit_grads]
        starts = 2 * main + at_other * rest
        rests = [g[:, starts : starts + rest] for g in unit_grads]
        blank = jnp.zeros((width, rest_lanes - 3 * rest), wide)
        return jnp.concatenate(mains + rests + [blank], axis=1)

    grad_set = (side_of(0) + net.swap(side_of(1).astype(low)).astype(wide)).astype(low)
    grad_set = grad_set.reshape(chips, rows, -1)
    got = net.exchange(lambda chip: lax.dynamic_index_in_dim(grad_set, chip, 0, keepdims=False))

    def unit_grad(at):
        start = 3 * main + at * rest
        main_part = jnp.transpose(got[:, :, at * main : (at + 1) * main], (1, 0, 2))
        rest_part = jnp.transpose(got[:, :, start : start + rest], (1, 0, 2))
        return jnp.concatenate(
            [main_part.reshape(rows, chips * main), rest_part.reshape(rows, chips * rest)], axis=1
        ).astype(wide)

    grad_gate, grad_up, grad_down = unit_grad(0), unit_grad(1), unit_grad(2)

    d_projected_all = jnp.concatenate(
        [g.reshape(-1, width) for g in net.gather_plane(d_projected_low, plane_groups)]
    )
    d_projected_asked = asked_rows(d_projected_all)
    d_mixed_low = product(d_projected_asked, w_out_head).astype(low)
    d_prob = product_right_t(d_mixed_low, all_values)
    delta = jnp.sum(probabilities * d_prob, axis=-1, keepdims=True)
    d_capped = probabilities * (d_prob - delta)
    d_scores = (d_capped * (1.0 - bent * bent)).astype(low)
    d_queries = product(d_scores, all_keys) * score_scale
    d_keys = product_left_t(d_scores, queries) * score_scale
    d_values = product_left_t(probabilities_low, d_mixed_low)
    d_kv = jnp.concatenate([d_keys, d_values], axis=1)
    count = places.shape[0]
    d_kv = d_kv[:count] + net.swap(d_kv[count:].astype(low)).astype(wide)
    d_query_low = turn(d_queries, asked_rows(cosine), -asked_rows(sine_part)).astype(low)
    d_key_low = turn(d_kv[:, :HEAD_DIM], cosine, -sine_part).astype(low)
    d_kv_low = jnp.concatenate([d_key_low, d_kv[:, HEAD_DIM:].astype(low)], axis=1)
    if asked is None:
        d_qkv_low = jnp.concatenate([d_query_low, d_kv_low], axis=1)
    else:
        blocks = jnp.zeros((2, net.ranks, half, HEAD_DIM), low)
        d_query_low = blocks.at[0, jnp.array(asked)].set(
            d_query_low.reshape(len(asked), half, HEAD_DIM)
        )
        d_qkv_low = jnp.concatenate([d_query_low.reshape(-1, HEAD_DIM), d_kv_low], axis=1)
    d_normed_part = product_right_t(d_qkv_low, w_qkv)
    grad_attn_in = jnp.sum(d_normed_part * units_in, axis=0)
    every = d_normed_part.astype(low)
    parts, start = [], 0
    for group in plane_groups:
        size = 2 * len(group) * half
        parts.append(every[start : start + size].reshape(2, len(group), half, width))
        start += size
    d_normed = net.scatter_plane(parts, plane_groups)
    own_inverse = inverse_size(own_inputs)
    own_grad = d_middle + norm_back(own_inputs * own_inverse, own_inverse, scale_in, d_normed)

    head_grads = jnp.concatenate(
        [
            product_left_t(normed_low, d_qkv_low),
            product_left_t(d_projected_asked, mixed_low),
        ],
        axis=1,
    ).reshape(chips, 2, cut_rows, 4 * HEAD_DIM)
    kept = lax.dynamic_index_in_dim(head_grads, core, 1, keepdims=False)
    given = lax.dynamic_index_in_dim(head_grads, 1 - core, 1, keepdims=False)
    head_grads = (kept + net.swap(given.astype(low)).astype(wide)).astype(low)
    got = net.exchange(lambda chip: lax.dynamic_index_in_dim(head_grads, chip, 0, keepdims=False))
    got = got.astype(wide).reshape(net.dp, net.context, cut_rows, 4 * HEAD_DIM)

    def heads_total(at, count_of):
        piece = got[..., at * HEAD_DIM : (at + 1) * HEAD_DIM]
        piece = piece.reshape(net.dp, count_of, -1, cut_rows, HEAD_DIM).sum(axis=(0, 2))
        return jnp.transpose(piece, (1, 0, 2)).reshape(cut_rows, 2, -1)

    whole = jnp.concatenate(
        [
            heads_total(0, heads),
            heads_total(1, kv_heads),
            heads_total(2, kv_heads),
            heads_total(3, heads),
        ],
        axis=2,
    )
    kept = lax.dynamic_index_in_dim(whole, core, 1, keepdims=False)
    given = lax.dynamic_index_in_dim(whole, 1 - core, 1, keepdims=False)
    upper, lower = net.ordered(kept, net.swap(given.astype(low)).astype(wide))
    whole = jnp.concatenate([upper, lower])
    grad_query = whole[:, edges[0] : edges[1]]
    grad_key = whole[:, edges[1] : edges[2]]
    grad_value = whole[:, edges[2] : edges[3]]
    grad_out = whole[:, edges[3] : edges[4]]

    gain_grads = jnp.stack([grad_attn_in, grad_attn_out, grad_ffw_in, grad_ffw_out])
    gain_grads = gain_grads + net.swap(gain_grads)
    gain_grads = jnp.transpose(gain_grads.reshape(4, chips, rows), (1, 0, 2))
    gain_grads = lax.all_to_all(gain_grads, chip_axes, 0, 0, tiled=True).sum(axis=0)

    layer_output = jnp.concatenate(net.ordered(own_output, net.swap(own_output)))
    input_grad = jnp.concatenate(net.ordered(own_grad, net.swap(own_grad)))
    return (
        layer_output[None],
        input_grad[None],
        grad_query,
        grad_key,
        grad_value,
        grad_out,
        grad_gate,
        grad_up,
        grad_down,
        gain_grads[0],
        gain_grads[1],
        gain_grads[2],
        gain_grads[3],
    )


def solution(mesh):
    tokens_spec = P("dp", "context", None)
    weight_spec = P(("dp", "context"), "tensor")
    gain_spec = P(("dp", "context"))
    return jax.shard_map(
        body,
        mesh=mesh,
        in_specs=(tokens_spec,) + (weight_spec,) * 7 + (gain_spec,) * 4 + (tokens_spec,),
        out_specs=(tokens_spec,) * 2 + (weight_spec,) * 7 + (gain_spec,) * 4,
        check_vma=False,
    )
```

```python
import jax
import jax.numpy as jnp
from jax import lax
from jax.experimental import pallas as pl
from jax.experimental.pallas import tpu as pltpu
from jax.sharding import PartitionSpec as P

HEAD_DIM = 256

epsilon = 1e-06
softcap = 50.0
theta = 10000.0
floor_value = -1e30
low = jnp.bfloat16
wide = jnp.float32
chip_axes = ("dp", "context")


def product(left_side, right_side):
    return jnp.dot(left_side, right_side, preferred_element_type=wide)


def product_right_t(left_side, right_side):
    return lax.dot_general(left_side, right_side, (((1,), (1,)), ((), ())), preferred_element_type=wide)


def product_left_t(left_side, right_side):
    return lax.dot_general(left_side, right_side, (((0,), (0,)), ((), ())), preferred_element_type=wide)


def inverse_size(values):
    return lax.rsqrt(jnp.mean(values * values, axis=-1, keepdims=True) + epsilon)


def norm_back(unit, inverse, scaling, upstream):
    inner = upstream * scaling
    return inverse * (inner - unit * jnp.mean(inner * unit, axis=-1, keepdims=True))


def turn(values, cosine, sine_part):
    half_width = values.shape[-1] // 2
    former = values[..., :half_width]
    latter = values[..., half_width:]
    return jnp.concatenate(
        [former * cosine - latter * sine_part, latter * cosine + former * sine_part], axis=-1
    )


def geglu(gate_in, upward):
    return jax.nn.gelu(gate_in, approximate=True) * upward


def pick(array, at, axis):
    return lax.dynamic_index_in_dim(array, at, axis, keepdims=False)


def hold(*trees):
    return lax.optimization_barrier(trees)


def placed(line, core, sources, rows):
    blocks, lanes = sources[0].shape[0], sources[0].shape[2]
    if rows % 16:
        ins = [source[:, :rows] for source in sources]
        lines = [
            jnp.stack([jnp.where(line == 0, a, b), jnp.where(line == 0, b, a)])
            for a, b in (ins[:2], ins[2:])
        ]
        return jnp.where(core == 0, lines[0], lines[1]), jnp.where(core == 0, lines[1], lines[0])

    def kernel(place_ref, *refs):
        ins, outs = refs[:4], refs[4:]
        for put in range(2):
            for at in range(2):
                chosen = (place_ref[0] ^ at) + 2 * (place_ref[1] ^ put)
                for number in range(4):

                    @pl.when(chosen == number)
                    def _(put=put, at=at, number=number):
                        outs[put][at] = ins[number][:, :rows]

    return pl.pallas_call(
        kernel,
        in_specs=[pl.BlockSpec(memory_space=pltpu.SMEM)] + [pl.BlockSpec(memory_space=pltpu.VMEM)] * 4,
        out_specs=[pl.BlockSpec(memory_space=pltpu.VMEM)] * 2,
        out_shape=[jax.ShapeDtypeStruct((2, blocks, rows, lanes), low)] * 2,
        compiler_params=pltpu.CompilerParams(vmem_limit_bytes=32 * 2**20),
        cost_estimate=pl.CostEstimate(
            flops=0, transcendentals=0, bytes_accessed=16 * blocks * rows * lanes
        ),
    )(jnp.stack([line, core]).astype(jnp.int32), *sources)


class Slice:
    def __init__(self):
        self.dp = lax.axis_size("dp")
        self.context = lax.axis_size("context")
        self.ranks = self.context // 2
        self.chips = self.dp * self.context
        self.core = lax.axis_index("tensor")
        self.place = lax.axis_index("context")
        self.rank = self.place // 2
        self.side = self.place % 2
        self.line = lax.axis_index("dp")

    def send(self, block, where):
        pairs = []
        for dp in range(self.dp):
            for rank in range(self.ranks):
                for side in range(2):
                    pairs.append(
                        (self.index(dp, rank, side), self.index(*where(dp, rank, side)))
                    )
        return lax.ppermute(block, chip_axes, pairs)

    def index(self, dp, rank, side):
        return (dp * self.ranks + rank % self.ranks) * 2 + side

    def across(self, block):
        return self.send(block, lambda dp, rank, side: (dp, rank, 1 - side))

    def over(self, block):
        return self.send(block, lambda dp, rank, side: (1 - dp, rank, side))

    def along(self, block, step):
        if step % self.ranks == 0:
            return block
        return self.send(block, lambda dp, rank, side: (dp, rank + step, side))

    def swap(self, block):
        return lax.ppermute(block, "tensor", [(0, 1), (1, 0)])

    def ordered(self, mine, other):
        first = self.core == 0
        return jnp.where(first, mine, other), jnp.where(first, other, mine)

    def moves(self, block):
        return [self.along(block, step) for step in range(self.ranks)]

    def returned(self, blocks):
        total = 0.0
        for step, block in enumerate(blocks):
            if step:
                block = self.along(block.astype(low), -step)
            total = total + block.astype(wide)
        return total

    def to_ranks(self, array):
        groups = [[rank * 2 + side for rank in range(self.ranks)] for side in range(2)]
        return lax.all_to_all(array, "context", 0, 0, tiled=True, axis_index_groups=groups)

    def square(self):
        return [
            [self.index(dp, rank, side) for dp in range(self.dp) for side in range(2)]
            for rank in range(self.ranks)
        ]

    def weights_in(self, array):
        ranks, rows, units = array.shape
        whole = lax.all_gather(array, chip_axes, axis=0, tiled=False, axis_index_groups=self.square())
        return whole.reshape(self.dp, 2, ranks, rows, units)

    def by_model_row(self, whole):
        return jnp.transpose(whole, (0, 2, 1, 3, 4)).reshape(-1, whole.shape[-1])

    def grads_out(self, grad, rows):
        units = grad.shape[1]
        parts = grad.astype(low).reshape(self.dp, self.ranks, 2, rows, units)
        parts = jnp.transpose(parts, (0, 2, 1, 3, 4)).reshape(-1, units)
        total = lax.psum_scatter(
            parts, chip_axes, scatter_dimension=0, tiled=True, axis_index_groups=self.square()
        )
        return total.reshape(self.ranks, rows, units)


def body(
    tokens,
    w_query,
    w_key,
    w_value,
    w_out,
    w_gate,
    w_up,
    w_down,
    gain_attn_in,
    gain_attn_out,
    gain_ffw_in,
    gain_ffw_out,
    cotangent,
):
    net = Slice()
    core, chips, ranks = net.core, net.chips, net.ranks
    span = tokens.shape[1]
    width = tokens.shape[2]
    half = span // 2
    rows = w_query.shape[0]
    heads = 2 * w_query.shape[1] // HEAD_DIM
    kv_heads = 2 * w_key.shape[1] // HEAD_DIM
    repeat = heads // kv_heads
    share = net.context // heads
    score_scale = HEAD_DIM ** (-0.5)
    units = w_gate.shape[1] // ranks
    q_cols, k_cols = w_query.shape[1], w_key.shape[1]
    is_front = core == 0

    own_tokens = lax.dynamic_slice_in_dim(tokens[0], core * half, half, 0)
    upstream = lax.dynamic_slice_in_dim(cotangent[0], core * half, half, 0)

    front = jnp.concatenate([w_query, w_key], axis=1)
    back = jnp.concatenate([w_out, w_value], axis=1)
    mine = jnp.where(is_front, front, back)
    theirs = net.swap(jnp.where(is_front, back, front))
    low_heads, high_heads = net.ordered(mine, theirs)

    def by_head(begin, end):
        both = jnp.concatenate([low_heads[:, begin:end], high_heads[:, begin:end]], axis=1)
        return jnp.transpose(both.reshape(rows, -1, HEAD_DIM), (1, 0, 2))

    gain_row = jnp.concatenate([gain_attn_in, gain_attn_out, gain_ffw_in, gain_ffw_out])
    gain_lanes = -(-4 * rows // (2 * HEAD_DIM))
    gain_row = jnp.pad(gain_row, (0, gain_lanes * 2 * HEAD_DIM - 4 * rows))
    gain_row = jnp.broadcast_to(
        gain_row.reshape(1, gain_lanes, 2 * HEAD_DIM), (heads, gain_lanes, 2 * HEAD_DIM)
    )
    head_sets = jnp.concatenate(
        [
            jnp.concatenate(
                [by_head(0, q_cols), jnp.repeat(by_head(q_cols, q_cols + k_cols), repeat, axis=0)],
                axis=2,
            ),
            gain_row,
        ],
        axis=1,
    )
    head_sets = jnp.repeat(head_sets, share, axis=0)
    part = lax.all_to_all(head_sets, "context", 0, 0, tiled=True)
    token_blocks = jnp.stack(net.moves(own_tokens))

    def by_rank(w):
        return jnp.transpose(w.reshape(rows, ranks, units), (1, 0, 2))

    gate_set, up_set, down_set = by_rank(w_gate), by_rank(w_up), by_rank(w_down)
    part, token_blocks, gate_set, up_set, down_set = hold(
        part, token_blocks, gate_set, up_set, down_set
    )
    token_blocks = jnp.stack([token_blocks, net.across(token_blocks)])
    part_line = net.over(part)
    gate_set = net.to_ranks(gate_set)
    token_blocks, part, part_line, gate_set, up_set = hold(
        token_blocks, part, part_line, gate_set, up_set
    )
    gate_units = net.weights_in(gate_set)
    up_set = net.to_ranks(up_set)

    part_core, part_both = net.swap(part), net.swap(part_line)
    front_weights, back_weights = placed(
        net.line, core, [part, part_line, part_core, part_both], rows
    )
    front_weights = front_weights.reshape(width, 2 * HEAD_DIM)
    back_weights = back_weights.reshape(width, 2 * HEAD_DIM)
    first_line = net.line == 0
    gain_own, gain_other = part[:, rows:], part_line[:, rows:]
    gain_rows = jnp.concatenate(
        [jnp.where(first_line, gain_own, gain_other), jnp.where(first_line, gain_other, gain_own)]
    ).reshape(chips, -1)
    gains = gain_rows[:, : 4 * rows].reshape(chips, 4, rows)
    gains = jnp.transpose(gains, (1, 0, 2)).reshape(4, width).astype(wide)
    scale_in, scale_mid, scale_pre, scale_out = gains[0], gains[1], gains[2], gains[3]
    w_out_head = back_weights[:, :HEAD_DIM]
    w_value_head = back_weights[:, HEAD_DIM:]

    own_inputs = own_tokens.astype(wide)
    inputs = token_blocks.reshape(-1, width).astype(wide)
    units_in = inputs * inverse_size(inputs)
    normed_low = (units_in * scale_in).astype(low)
    block_places = jnp.concatenate(
        [(net.rank - jnp.arange(ranks)) % ranks * 2 + side for side in (net.side, 1 - net.side)]
    )
    offsets = jnp.arange(half, dtype=jnp.int32)
    places = (block_places[:, None] * span + core * half + offsets[None, :]).reshape(-1)
    other_places = places + (1 - 2 * core) * half
    exponent = jnp.arange(HEAD_DIM // 2, dtype=wide) * (-2.0 / HEAD_DIM)
    angles = places.astype(wide)[:, None] * (theta**exponent)[None, :]
    cosine, sine_part = jnp.cos(angles), jnp.sin(angles)
    asked = tuple(range(0, ranks, max(share // 2, 1)))

    def asked_rows(array):
        if share == 1:
            return array
        blocks = array.reshape((2, ranks, half) + array.shape[1:])
        return jnp.concatenate([blocks[0, step] for step in asked])

    query_key = product(normed_low, front_weights)
    queries = asked_rows(turn(query_key[:, :HEAD_DIM], cosine, sine_part).astype(low))
    keys = turn(query_key[:, HEAD_DIM:], cosine, sine_part).astype(low)
    values = product(normed_low, w_value_head).astype(low)
    own_kv = jnp.concatenate([keys, values], axis=1)
    all_kv = jnp.concatenate([own_kv, net.swap(own_kv)])
    all_keys, all_values = all_kv[:, :HEAD_DIM], all_kv[:, HEAD_DIM:]
    key_places = jnp.concatenate([places, other_places])
    allowed = key_places[None, :] <= asked_rows(places)[:, None]
    scores = product_right_t(queries, all_keys) * score_scale
    bent = jnp.tanh(scores / softcap)
    capped = jnp.where(allowed, softcap * bent, floor_value)
    shifted = jnp.exp(capped - jnp.max(capped, axis=-1, keepdims=True))
    probabilities = shifted / jnp.sum(shifted, axis=-1, keepdims=True)
    probabilities_low = probabilities.astype(low)
    mixed_low = product(probabilities_low, all_values).astype(low)
    out_parts = product_right_t(mixed_low, w_out_head).astype(low)
    out_parts, up_set, down_set = hold(out_parts, up_set, down_set)
    up_units = net.weights_in(up_set)
    down_set = net.to_ranks(down_set)
    if share == 1:
        out_parts = out_parts.reshape(2, ranks, half, width)
        out_parts = out_parts[0].astype(wide) + net.across(out_parts[1]).astype(wide)
    else:
        out_parts = out_parts.reshape(len(asked), half, width).astype(wide)
    projected = 0.0
    for at, step in enumerate(asked):
        block = out_parts[at]
        if step:
            block = net.along(block.astype(low), -step).astype(wide)
        projected = projected + block

    projected, down_set = hold(projected, down_set)
    down_units = net.weights_in(down_set)

    inverse_mid = inverse_size(projected)
    unit_mid = projected * inverse_mid
    middle = own_inputs + unit_mid * scale_mid
    inverse_pre = inverse_size(middle)
    unit_pre = middle * inverse_pre
    normed_two_low = (unit_pre * scale_pre).astype(low)
    two_blocks = jnp.stack(net.moves(normed_two_low)).reshape(-1, width)
    two_blocks, gate_units, up_units = hold(two_blocks, gate_units, up_units)
    pair_units = jnp.concatenate([net.by_model_row(gate_units), net.by_model_row(up_units)], axis=1)

    all_two = jnp.concatenate([two_blocks, net.swap(two_blocks)])
    pair = product(all_two, pair_units)
    gate_in, upward = pair[:, :units], pair[:, units:]
    hidden_low = geglu(gate_in, upward).astype(low)
    hidden_low, down_units = hold(hidden_low, down_units)
    down_units = net.by_model_row(down_units)

    def core_total(part):
        count = ranks * half
        part = part.astype(low)
        return part[:count].astype(wide) + net.swap(part[count:]).astype(wide)

    def line_total(own):
        return net.returned(list(own.reshape(ranks, half, width)))

    branch = line_total(core_total(product_right_t(hidden_low, down_units)))
    inverse_out = inverse_size(branch)
    unit_out = branch * inverse_out
    own_output = (middle + unit_out * scale_out).astype(low)

    grad_ffw_out = jnp.sum(upstream * unit_out, axis=0)
    d_branch_low = norm_back(unit_out, inverse_out, scale_out, upstream).astype(low)
    branch_blocks = jnp.stack(net.moves(d_branch_low)).reshape(-1, width)
    all_branch = jnp.concatenate([branch_blocks, net.swap(branch_blocks)])

    down_grad = product_left_t(all_branch, hidden_low).astype(low)
    down_grad, all_branch = hold(down_grad, all_branch)
    down_grad = net.grads_out(down_grad, rows)
    d_hidden = product(all_branch, down_units)
    _, pull = jax.vjp(geglu, gate_in, upward)
    d_gate, d_up = pull(d_hidden)
    d_pair_low = jnp.concatenate([d_gate.astype(low), d_up.astype(low)], axis=1)
    d_two = core_total(product_right_t(d_pair_low, pair_units))
    d_normed_two = line_total(d_two)
    d_normed_two, d_pair_low, all_two = hold(d_normed_two, d_pair_low, all_two)
    pair_grad = product_left_t(all_two, d_pair_low).astype(low)
    gate_grad = net.grads_out(pair_grad[:, :units], rows)
    up_grad = pair_grad[:, units:]
    gate_grad, up_grad = hold(gate_grad, up_grad)
    up_grad = net.grads_out(up_grad, rows)
    grad_ffw_in = jnp.sum(d_normed_two * unit_pre, axis=0)
    d_middle = upstream + norm_back(unit_pre, inverse_pre, scale_pre, d_normed_two)
    grad_attn_out = jnp.sum(d_middle * unit_mid, axis=0)
    d_projected_low = norm_back(unit_mid, inverse_mid, scale_mid, d_middle).astype(low)
    d_projected_all = jnp.stack(net.moves(d_projected_low))
    d_projected_all, down_grad = hold(d_projected_all, down_grad)
    down_grad = net.to_ranks(down_grad)
    d_projected_all = jnp.stack([d_projected_all, net.across(d_projected_all)]).reshape(-1, width)
    d_projected_asked = asked_rows(d_projected_all)
    d_mixed_low = product(d_projected_asked, w_out_head).astype(low)
    d_prob = product_right_t(d_mixed_low, all_values)
    delta = jnp.sum(probabilities * d_prob, axis=-1, keepdims=True)
    d_capped = probabilities * (d_prob - delta)
    d_scores = (d_capped * (1.0 - bent * bent)).astype(low)
    d_queries = product(d_scores, all_keys) * score_scale
    d_keys = product_left_t(d_scores, queries) * score_scale
    d_values = product_left_t(probabilities_low, d_mixed_low)
    d_kv = jnp.concatenate([d_keys, d_values], axis=1)
    count = places.shape[0]
    d_kv = d_kv[:count] + net.swap(d_kv[count:].astype(low)).astype(wide)
    d_query_low = turn(d_queries, asked_rows(cosine), -asked_rows(sine_part)).astype(low)
    d_key_low = turn(d_kv[:, :HEAD_DIM], cosine, -sine_part).astype(low)
    if share != 1:
        blocks = jnp.zeros((2, ranks, half, HEAD_DIM), low)
        d_query_low = blocks.at[0, jnp.array(asked)].set(
            d_query_low.reshape(len(asked), half, HEAD_DIM)
        )
        d_query_low = d_query_low.reshape(-1, HEAD_DIM)
    d_value_low = d_kv[:, HEAD_DIM:].astype(low)
    d_front_low = jnp.concatenate([d_query_low, d_key_low], axis=1)
    d_normed_part = product_right_t(d_front_low, front_weights)
    d_normed_part = d_normed_part + product_right_t(d_value_low, w_value_head)
    grad_attn_in = jnp.sum(d_normed_part * units_in, axis=0)
    d_normed_low = d_normed_part.astype(low).reshape(2, ranks, half, width)
    gate_grad, down_grad, d_normed_low, d_front_low, d_value_low = hold(
        gate_grad, down_grad, d_normed_low, d_front_low, d_value_low
    )
    gate_grad = net.to_ranks(gate_grad)
    d_normed = d_normed_low[0].astype(wide) + net.across(d_normed_low[1]).astype(wide)
    d_normed, gate_grad = hold(d_normed, gate_grad)
    front_grads = product_left_t(normed_low, d_front_low)
    back_grads = jnp.concatenate(
        [
            product_left_t(d_projected_asked, mixed_low),
            product_left_t(normed_low, d_value_low),
        ],
        axis=1,
    )
    given = jnp.where(is_front, back_grads, front_grads).astype(low)
    kept = jnp.where(is_front, front_grads, back_grads)
    kept = (kept + net.swap(given).astype(wide)).astype(low)
    kept = kept.reshape(net.dp, net.context, rows, 2 * HEAD_DIM)
    d_normed = net.returned(list(d_normed))

    def line_sum(array):
        return pick(array, net.line, 0).astype(wide) + net.over(pick(array, 1 - net.line, 0)).astype(wide)

    gain_grads = jnp.stack([grad_attn_in, grad_attn_out, grad_ffw_in, grad_ffw_out])
    gain_grads = gain_grads + net.swap(gain_grads)
    gain_grads = jnp.transpose(gain_grads.reshape(4, net.dp, net.context, rows), (1, 2, 0, 3))
    gain_grads = line_sum(gain_grads.reshape(net.dp, net.context, 4 * rows))
    gain_grads = jnp.pad(gain_grads, ((0, 0), (0, gain_lanes * 2 * HEAD_DIM - 4 * rows)))
    gain_grads = gain_grads.reshape(net.context, gain_lanes, 2 * HEAD_DIM)
    gain_high = gain_grads.astype(low)
    gain_low = (gain_grads - gain_high.astype(wide)).astype(low)
    head_grads = jnp.concatenate([line_sum(kept).astype(low), gain_high, gain_low], axis=1)
    own_inverse = inverse_size(own_inputs)
    own_grad = d_middle + norm_back(own_inputs * own_inverse, own_inverse, scale_in, d_normed)
    layer_output = jnp.concatenate(net.ordered(own_output, net.swap(own_output)))
    input_grad = jnp.concatenate(net.ordered(own_grad, net.swap(own_grad)))
    got = lax.all_to_all(head_grads, "context", 0, 0, tiled=True)
    got, up_grad = hold(got, up_grad)
    up_grad = net.to_ranks(up_grad)
    got = got.astype(wide)
    gain_got = got[:, rows:].reshape(net.context, 2, -1).sum(axis=(0, 1))
    gain_got = gain_got[: 4 * rows].reshape(4, rows)

    def heads_total(at, count_of):
        piece = got[:, :rows, at * HEAD_DIM : (at + 1) * HEAD_DIM]
        piece = piece.reshape(count_of, -1, rows, HEAD_DIM).sum(axis=1)
        return jnp.transpose(piece, (1, 0, 2)).reshape(rows, 2, -1)

    total = jnp.concatenate([heads_total(0, heads), heads_total(1, kv_heads)], axis=2)
    kept = pick(total, core, 1)
    given = pick(total, 1 - core, 1)
    front, back = net.ordered(kept, net.swap(given.astype(low)).astype(wide))
    grad_query, grad_key = front[:, :q_cols], front[:, q_cols:]
    grad_out, grad_value = back[:, :q_cols], back[:, q_cols:]

    def by_units(pieces):
        return jnp.transpose(pieces, (1, 0, 2)).reshape(rows, ranks * units).astype(wide)

    return (
        layer_output[None],
        input_grad[None],
        grad_query,
        grad_key,
        grad_value,
        grad_out,
        by_units(gate_grad),
        by_units(up_grad),
        by_units(down_grad),
        gain_got[0],
        gain_got[1],
        gain_got[2],
        gain_got[3],
    )


def solution(mesh):
    tokens_spec = P("dp", "context", None)
    weight_spec = P(("dp", "context"), "tensor")
    gain_spec = P(("dp", "context"))
    return jax.shard_map(
        body,
        mesh=mesh,
        in_specs=(tokens_spec,) + (weight_spec,) * 7 + (gain_spec,) * 4 + (tokens_spec,),
        out_specs=(tokens_spec,) * 2 + (weight_spec,) * 7 + (gain_spec,) * 4,
        check_vma=False,
    )
```

```python
import jax
import jax.numpy as jnp
from jax import lax
from jax.experimental import pallas as pl
from jax.experimental.pallas import tpu as pltpu
from jax.sharding import PartitionSpec as P

HEAD_DIM = 256
LANES = 128
LANES = 128

epsilon = 1e-06
softcap = 50.0
theta = 10000.0
floor_value = -1e30
low = jnp.bfloat16
wide = jnp.float32
chip_axes = ("dp", "context")
all_axes = ("dp", "context", "tensor")


def product(left_side, right_side):
    return jnp.dot(left_side, right_side, preferred_element_type=wide)


def product_right_t(left_side, right_side):
    return lax.dot_general(left_side, right_side, (((1,), (1,)), ((), ())), preferred_element_type=wide)


def product_left_t(left_side, right_side):
    return lax.dot_general(left_side, right_side, (((0,), (0,)), ((), ())), preferred_element_type=wide)


def inverse_size(values):
    return lax.rsqrt(jnp.mean(values * values, axis=-1, keepdims=True) + epsilon)


def norm_back(unit, inverse, scaling, upstream):
    inner = upstream * scaling
    return inverse * (inner - unit * jnp.mean(inner * unit, axis=-1, keepdims=True))


def turn(values, cosine, sine_part):
    half_width = values.shape[-1] // 2
    former = values[..., :half_width]
    latter = values[..., half_width:]
    return jnp.concatenate(
        [former * cosine - latter * sine_part, latter * cosine + former * sine_part], axis=-1
    )


def geglu(gate_in, upward):
    return jax.nn.gelu(gate_in, approximate=True) * upward


def pick(array, at, axis):
    return lax.dynamic_index_in_dim(array, at, axis, keepdims=False)


def hold(*trees):
    return lax.optimization_barrier(trees)


def assembled(place, ranks, rows, upper, lower, others):
    count, units = len(others), others[0].shape[3]
    parts = upper.shape[3], lower.shape[3]

    def kernel(place_ref, upper_ref, lower_ref, *refs):
        out, own = refs[-1], place_ref[2]
        for at in range(count):
            begin = at * units
            out[0, own, 0, :, begin : begin + parts[0]] = upper_ref[0, at]
            out[0, own, 0, :, begin + parts[0] : begin + units] = lower_ref[0, at]
            for step in range(1, ranks):
                out[0, (own + step) % ranks, 0, :, begin : begin + units] = refs[at][0, step - 1]

    def relative(line, side, place):
        return ((line ^ place[0]) * 2 + (side ^ place[1]), 0, 0, 0)

    whole = pl.pallas_call(
        kernel,
        grid_spec=pltpu.PrefetchScalarGridSpec(
            num_scalar_prefetch=1,
            grid=(2, 2),
            in_specs=[
                pl.BlockSpec((1, count, rows, parts[0]), relative),
                pl.BlockSpec((1, count, rows, parts[1]), relative),
            ]
            + [
                pl.BlockSpec(
                    (1, ranks - 1, rows, units), lambda line, side, place: (line * 2 + side, 0, 0, 0)
                )
            ]
            * count,
            out_specs=pl.BlockSpec(
                (1, ranks, 1, rows, count * units), lambda line, side, place: (line, 0, side, 0, 0)
            ),
        ),
        out_shape=jax.ShapeDtypeStruct((2, ranks, 2, rows, count * units), low),
        compiler_params=pltpu.CompilerParams(vmem_limit_bytes=32 * 2**20),
        cost_estimate=pl.CostEstimate(
            flops=0, transcendentals=0, bytes_accessed=16 * ranks * rows * count * units
        ),
    )(place, upper, lower, *others)
    return whole.reshape(-1, count * units)


class Slice:
    def __init__(self):
        self.dp = lax.axis_size("dp")
        self.context = lax.axis_size("context")
        self.ranks = self.context // 2
        self.chips = self.dp * self.context
        self.core = lax.axis_index("tensor")
        self.place = lax.axis_index("context")
        self.rank = self.place // 2
        self.side = self.place % 2
        self.line = lax.axis_index("dp")

    def send(self, block, where):
        pairs = []
        for dp in range(self.dp):
            for rank in range(self.ranks):
                for side in range(2):
                    pairs.append(
                        (self.index(dp, rank, side), self.index(*where(dp, rank, side)))
                    )
        return lax.ppermute(block, chip_axes, pairs)

    def index(self, dp, rank, side):
        return (dp * self.ranks + rank % self.ranks) * 2 + side

    def across(self, block):
        return self.send(block, lambda dp, rank, side: (dp, rank, 1 - side))

    def over(self, block):
        return self.send(block, lambda dp, rank, side: (1 - dp, rank, side))

    def along(self, block, step):
        if step % self.ranks == 0:
            return block
        return self.send(block, lambda dp, rank, side: (dp, rank + step, side))

    def swap(self, block):
        return lax.ppermute(block, "tensor", [(0, 1), (1, 0)])

    def ordered(self, mine, other):
        first = self.core == 0
        return jnp.where(first, mine, other), jnp.where(first, other, mine)

    def moves(self, block):
        return [self.along(block, step) for step in range(self.ranks)]

    def returned(self, blocks):
        total = 0.0
        for step, block in enumerate(blocks):
            if step:
                block = self.along(block.astype(low), -step)
            total = total + block.astype(wide)
        return total

    def to_ranks(self, array):
        groups = [[rank * 2 + side for rank in range(self.ranks)] for side in range(2)]
        return lax.all_to_all(array, "context", 0, 0, tiled=True, axis_index_groups=groups)

    def square(self):
        return [
            [self.index(dp, rank, side) for dp in range(self.dp) for side in range(2)]
            for rank in range(self.ranks)
        ]

    def square_cores(self):
        return [[2 * chip + core for chip in chips for core in range(2)] for chips in self.square()]

    def heads_in(self, array):
        whole = lax.all_gather(
            array, all_axes, axis=0, tiled=False, axis_index_groups=self.square_cores()
        )
        return whole.reshape((self.dp, 2, 2) + array.shape)

    def heads_by_square(self, grads, rows):
        lanes = grads[0].shape[1]
        parts = [g.astype(low).reshape(self.dp, self.ranks, 2, rows, lanes) for g in grads]
        parts = [jnp.transpose(part, (0, 2, 1, 3, 4)) for part in parts]
        return jnp.stack(parts, axis=2).reshape(-1, lanes)

    def head_grads_out(self, parts, rows):
        total = lax.psum_scatter(
            parts,
            all_axes,
            scatter_dimension=0,
            tiled=True,
            axis_index_groups=self.square_cores(),
        )
        return total.reshape(self.ranks, rows, -1)

    def weights_in(self, array):
        ranks, rows, units = array.shape
        whole = lax.all_gather(array, chip_axes, axis=0, tiled=False, axis_index_groups=self.square())
        return whole.reshape(self.dp, 2, ranks, rows, units)

    def others_in(self, array):
        ranks = array.shape[0]
        around = jnp.concatenate([array, array[: ranks - 1]])
        around = lax.dynamic_slice_in_dim(around, self.rank + 1, ranks - 1, 0)
        return lax.all_gather(
            around, chip_axes, axis=0, tiled=False, axis_index_groups=self.square()
        )

    def by_model_row(self, whole):
        return jnp.transpose(whole, (0, 2, 1, 3, 4)).reshape(-1, whole.shape[-1])

    def by_square(self, grad, rows):
        parts = grad.astype(low).reshape(self.dp, self.ranks, 2, rows, -1)
        return jnp.transpose(parts, (0, 2, 1, 3, 4)).reshape(-1, grad.shape[1])

    def grads_out(self, parts, rows):
        total = lax.psum_scatter(
            parts, chip_axes, scatter_dimension=0, tiled=True, axis_index_groups=self.square()
        )
        return total.reshape(self.ranks, rows, -1)


def body(
    tokens,
    w_query,
    w_key,
    w_value,
    w_out,
    w_gate,
    w_up,
    w_down,
    gain_attn_in,
    gain_attn_out,
    gain_ffw_in,
    gain_ffw_out,
    cotangent,
):
    net = Slice()
    core, chips, ranks = net.core, net.chips, net.ranks
    span = tokens.shape[1]
    width = tokens.shape[2]
    half = span // 2
    rows = w_query.shape[0]
    heads = 2 * w_query.shape[1] // HEAD_DIM
    kv_heads = 2 * w_key.shape[1] // HEAD_DIM
    repeat = heads // kv_heads
    share = ranks // kv_heads
    score_scale = HEAD_DIM ** (-0.5)
    units = w_gate.shape[1] // ranks
    q_cols, k_cols = w_query.shape[1], w_key.shape[1]
    is_front = core == 0

    own_tokens = lax.dynamic_slice_in_dim(tokens[0], core * half, half, 0)
    upstream = lax.dynamic_slice_in_dim(cotangent[0], core * half, half, 0)

    front = jnp.concatenate([w_query, w_key], axis=1)
    back = jnp.concatenate([w_out, w_value], axis=1)
    mine = jnp.where(is_front, front, back)
    theirs = net.swap(jnp.where(is_front, back, front))
    low_heads, high_heads = net.ordered(mine, theirs)

    def by_group(begin, end):
        both = jnp.concatenate([low_heads[:, begin:end], high_heads[:, begin:end]], axis=1)
        return jnp.transpose(both.reshape(rows, kv_heads, -1), (1, 0, 2))

    lanes = (repeat + 1) * HEAD_DIM
    gain_row = jnp.concatenate([gain_attn_in, gain_attn_out, gain_ffw_in, gain_ffw_out])
    gain_row = jnp.pad(gain_row, (0, lanes - 4 * rows))
    head_sets = jnp.concatenate([by_group(0, q_cols), by_group(q_cols, q_cols + k_cols)], axis=2)
    head_sets = jnp.concatenate(
        [head_sets, jnp.broadcast_to(gain_row, (kv_heads, 1, lanes))], axis=1
    )
    part = net.to_ranks(jnp.repeat(head_sets, share, axis=0))

    def by_rank(w):
        return jnp.transpose(w.reshape(rows, ranks, units), (1, 0, 2))

    gate_set, up_set, down_set = by_rank(w_gate), by_rank(w_up), by_rank(w_down)
    token_blocks = jnp.stack(net.moves(own_tokens))

    by_parts = rows % 16 == 0 and units % LANES == 0
    if by_parts:
        own_units = jnp.stack(
            [lax.dynamic_slice_in_dim(w, net.rank * units, units, 1) for w in (w_gate, w_up, w_down)]
        )
        middle_lane = (units // LANES + 1) // 2 * LANES
        upper, lower = own_units[:, :, :middle_lane], own_units[:, :, middle_lane:]
        upper = jnp.stack([upper, net.across(upper)])
        lower = jnp.stack([lower, net.over(lower)])
        part, token_blocks, upper, lower, gate_set, up_set, down_set = hold(
            part, token_blocks, upper, lower, gate_set, up_set, down_set
        )
        upper = jnp.concatenate([upper, net.over(upper)])
        lower_side = net.across(lower)
        lower = jnp.stack([lower[0], lower_side[0], lower[1], lower_side[1]])
        place = jnp.stack([net.line, net.side, net.rank]).astype(jnp.int32)
    else:
        part, token_blocks, gate_set, up_set, down_set = hold(
            part, token_blocks, gate_set, up_set, down_set
        )
    weights_in = net.others_in if by_parts else net.weights_in

    gate_set = net.to_ranks(gate_set)
    head_all = net.heads_in(part)
    gate_units = weights_in(gate_set)
    gate_set, up_set = hold(gate_set, up_set)
    up_set = net.to_ranks(up_set)
    up_units = weights_in(up_set)
    up_set, down_set = hold(up_set, down_set)
    down_set = net.to_ranks(down_set)
    down_units = weights_in(down_set)

    own_inputs = own_tokens.astype(wide)
    block_places = (net.rank - jnp.arange(ranks)) % ranks * 2 * span
    offsets = jnp.arange(half, dtype=jnp.int32)
    line_places = (block_places[:, None] + offsets[None, :]).reshape(-1)
    places = line_places + net.side * span + core * half
    key_places = jnp.concatenate(
        [
            line_places + side * span + of * half
            for side in (net.side, 1 - net.side)
            for of in (core, 1 - core)
        ]
    )
    exponent = jnp.arange(HEAD_DIM // 2, dtype=wide) * (-2.0 / HEAD_DIM)
    angles = places.astype(wide)[:, None] * (theta**exponent)[None, :]
    cosine, sine_part = jnp.cos(angles), jnp.sin(angles)
    asked = tuple(range(0, ranks, share))

    def asked_rows(array):
        if share == 1:
            return array
        blocks = array.reshape((ranks, half) + array.shape[1:])
        return jnp.concatenate([blocks[step] for step in asked])

    def by_head(array):
        return jnp.concatenate(jnp.split(array, repeat, axis=1))

    def by_token(array):
        return jnp.concatenate(jnp.split(array, repeat), axis=1)

    cosine_heads = jnp.concatenate([asked_rows(cosine)] * repeat)
    sine_heads = jnp.concatenate([asked_rows(sine_part)] * repeat)
    head_cols = repeat * HEAD_DIM

    def attend(head_all, token_blocks):
        front_weights = net.by_model_row(head_all[:, :, 0, :, :rows])
        back_weights = net.by_model_row(head_all[:, :, 1, :, :rows])
        gains = jnp.transpose(head_all[:, :, 0, :, rows, : 4 * rows], (0, 2, 1, 3))
        gains = jnp.transpose(gains.reshape(chips, 4, rows), (1, 0, 2)).reshape(4, width).astype(wide)
        inputs = token_blocks.reshape(-1, width).astype(wide)
        normed_low = (inputs * inverse_size(inputs) * gains[0]).astype(low)
        query_key = product(normed_low, front_weights)
        queries = turn(by_head(asked_rows(query_key[:, :head_cols])), cosine_heads, sine_heads)
        queries = queries.astype(low)
        keys = turn(query_key[:, head_cols:], cosine, sine_part).astype(low)
        values = product(normed_low, back_weights[:, head_cols:]).astype(low)
        own_kv = jnp.concatenate([keys, values], axis=1)
        side_kv = jnp.stack([own_kv, net.swap(own_kv)])
        all_kv = jnp.concatenate([side_kv, net.across(side_kv)]).reshape(-1, 2 * HEAD_DIM)
        allowed = key_places[None, :] <= jnp.concatenate([asked_rows(places)] * repeat)[:, None]
        scores = product_right_t(queries, all_kv[:, :HEAD_DIM]) * score_scale
        bent = jnp.tanh(scores / softcap)
        capped = jnp.where(allowed, softcap * bent, floor_value)
        shifted = jnp.exp(capped - jnp.max(capped, axis=-1, keepdims=True))
        probabilities = shifted / jnp.sum(shifted, axis=-1, keepdims=True)
        mixed = product(probabilities.astype(low), all_kv[:, HEAD_DIM:])
        mixed_low = by_token(mixed.astype(low))
        out_parts = product_right_t(mixed_low, back_weights[:, :head_cols]).astype(low)
        return (
            front_weights,
            back_weights,
            gains,
            normed_low,
            queries,
            all_kv,
            probabilities,
            bent,
            mixed_low,
            out_parts,
        )

    (
        front_weights,
        back_weights,
        gains,
        normed_low,
        queries,
        all_kv,
        probabilities,
        bent,
        mixed_low,
        out_parts,
    ) = attend(head_all, token_blocks)
    scale_in, scale_mid, scale_pre, scale_out = gains[0], gains[1], gains[2], gains[3]
    w_out_head = back_weights[:, :head_cols]
    w_value_head = back_weights[:, head_cols:]
    all_keys, all_values = all_kv[:, :HEAD_DIM], all_kv[:, HEAD_DIM:]
    probabilities_low = probabilities.astype(low)
    inputs = token_blocks.reshape(-1, width).astype(wide)
    units_in = inputs * inverse_size(inputs)
    out_parts = out_parts.reshape(len(asked), half, width).astype(wide)
    projected = 0.0
    for at, step in enumerate(asked):
        block = out_parts[at]
        if step:
            block = net.along(block.astype(low), -step).astype(wide)
        projected = projected + block


    inverse_mid = inverse_size(projected)
    unit_mid = projected * inverse_mid
    middle = own_inputs + unit_mid * scale_mid
    inverse_pre = inverse_size(middle)
    unit_pre = middle * inverse_pre
    normed_two_low = (unit_pre * scale_pre).astype(low)
    two_blocks = jnp.stack(net.moves(normed_two_low)).reshape(-1, width)
    two_blocks, gate_units, up_units = hold(two_blocks, gate_units, up_units)
    if by_parts:
        pair_units = assembled(place, ranks, rows, upper[:, :2], lower[:, :2], [gate_units, up_units])
    else:
        pair_units = jnp.concatenate(
            [net.by_model_row(gate_units), net.by_model_row(up_units)], axis=1
        )

    all_two = jnp.concatenate([two_blocks, net.swap(two_blocks)])
    pair = product(all_two, pair_units)
    gate_in, upward = pair[:, :units], pair[:, units:]
    hidden_low = geglu(gate_in, upward).astype(low)
    hidden_low, down_units = hold(hidden_low, down_units)
    if by_parts:
        down_units = assembled(place, ranks, rows, upper[:, 2:], lower[:, 2:], [down_units])
    else:
        down_units = net.by_model_row(down_units)

    def core_total(part):
        count = ranks * half
        part = part.astype(low)
        return part[:count].astype(wide) + net.swap(part[count:]).astype(wide)

    def line_total(own):
        return net.returned(list(own.reshape(ranks, half, width)))

    branch = line_total(core_total(product_right_t(hidden_low, down_units)))
    inverse_out = inverse_size(branch)
    unit_out = branch * inverse_out
    own_output = (middle + unit_out * scale_out).astype(low)

    grad_ffw_out = jnp.sum(upstream * unit_out, axis=0)
    d_branch_low = norm_back(unit_out, inverse_out, scale_out, upstream).astype(low)
    branch_blocks = jnp.stack(net.moves(d_branch_low)).reshape(-1, width)
    all_branch = jnp.concatenate([branch_blocks, net.swap(branch_blocks)])

    down_grad = net.by_square(product_left_t(all_branch, hidden_low), rows)
    down_grad, all_branch = hold(down_grad, all_branch)
    down_grad = net.grads_out(down_grad, rows)
    d_hidden = product(all_branch, down_units)
    _, pull = jax.vjp(geglu, gate_in, upward)
    d_gate, d_up = pull(d_hidden)
    d_pair_low = jnp.concatenate([d_gate.astype(low), d_up.astype(low)], axis=1)
    d_two = core_total(product_right_t(d_pair_low, pair_units))
    d_normed_two = line_total(d_two)
    pair_grad = net.by_square(product_left_t(all_two, d_pair_low), rows)
    d_normed_two, pair_grad = hold(d_normed_two, pair_grad)
    pair_grad = net.grads_out(pair_grad, rows)
    grad_ffw_in = jnp.sum(d_normed_two * unit_pre, axis=0)
    d_middle = upstream + norm_back(unit_pre, inverse_pre, scale_pre, d_normed_two)
    grad_attn_out = jnp.sum(d_middle * unit_mid, axis=0)
    d_projected_low = norm_back(unit_mid, inverse_mid, scale_mid, d_middle).astype(low)
    d_projected_all = jnp.stack(net.moves(d_projected_low))
    d_projected_all, down_grad = hold(d_projected_all, down_grad)
    down_grad = net.to_ranks(down_grad)
    d_projected_asked = asked_rows(d_projected_all.reshape(-1, width))
    d_mixed_low = by_head(product(d_projected_asked, w_out_head).astype(low))
    d_prob = product_right_t(d_mixed_low, all_values)
    delta = jnp.sum(probabilities * d_prob, axis=-1, keepdims=True)
    d_capped = probabilities * (d_prob - delta)
    d_scores = (d_capped * (1.0 - bent * bent)).astype(low)
    d_queries = product(d_scores, all_keys) * score_scale
    d_keys = product_left_t(d_scores, queries) * score_scale
    d_values = product_left_t(probabilities_low, d_mixed_low)
    d_kv = jnp.concatenate([d_keys, d_values], axis=1)
    d_kv = d_kv.reshape(2, 2, ranks * half, 2 * HEAD_DIM)
    d_kv = d_kv[0] + net.across(d_kv[1].astype(low)).astype(wide)
    d_kv = d_kv[0] + net.swap(d_kv[1].astype(low)).astype(wide)
    d_query_low = by_token(turn(d_queries, cosine_heads, -sine_heads).astype(low))
    d_key_low = turn(d_kv[:, :HEAD_DIM], cosine, -sine_part).astype(low)
    if share != 1:
        blocks = jnp.zeros((ranks, half, repeat * HEAD_DIM), low)
        d_query_low = blocks.at[jnp.array(asked)].set(
            d_query_low.reshape(len(asked), half, repeat * HEAD_DIM)
        )
        d_query_low = d_query_low.reshape(-1, repeat * HEAD_DIM)
    d_value_low = d_kv[:, HEAD_DIM:].astype(low)
    d_front_low = jnp.concatenate([d_query_low, d_key_low], axis=1)
    d_normed_part = product_right_t(d_front_low, front_weights)
    d_normed_part = d_normed_part + product_right_t(d_value_low, w_value_head)
    grad_attn_in = jnp.sum(d_normed_part * units_in, axis=0)
    d_normed_low = d_normed_part.astype(low).reshape(ranks, half, width)
    down_grad, d_normed_low, d_front_low, d_value_low = hold(
        down_grad, d_normed_low, d_front_low, d_value_low
    )
    d_normed = net.returned(list(d_normed_low))
    front_grads = product_left_t(normed_low, d_front_low)
    back_grads = jnp.concatenate(
        [
            product_left_t(d_projected_asked, mixed_low),
            product_left_t(normed_low, d_value_low),
        ],
        axis=1,
    )
    head_grads = net.heads_by_square([front_grads, back_grads], rows)
    d_normed, pair_grad, head_grads = hold(d_normed, pair_grad, head_grads)
    head_grads = net.head_grads_out(head_grads, rows)
    pair_grad = net.to_ranks(pair_grad)
    gain_grads = jnp.stack([grad_attn_in, grad_attn_out, grad_ffw_in, grad_ffw_out])
    gain_grads = gain_grads + net.swap(gain_grads)
    gain_grads = jnp.transpose(gain_grads.reshape(4, net.dp, ranks, 2, rows), (1, 2, 3, 0, 4))
    gain_grads = pick(gain_grads, net.line, 0) + net.over(pick(gain_grads, 1 - net.line, 0))
    gain_grads = pick(gain_grads, net.side, 1) + net.across(pick(gain_grads, 1 - net.side, 1))
    gain_got = pick(gain_grads, net.rank, 0)
    for step in range(1, ranks):
        gain_got = gain_got + net.along(pick(gain_grads, (net.rank + step) % ranks, 0), step)
    own_inverse = inverse_size(own_inputs)
    own_grad = d_middle + norm_back(own_inputs * own_inverse, own_inverse, scale_in, d_normed)
    layer_output = jnp.concatenate(net.ordered(own_output, net.swap(own_output)))
    input_grad = jnp.concatenate(net.ordered(own_grad, net.swap(own_grad)))
    pair_grad, head_grads = hold(pair_grad, head_grads)
    got = net.to_ranks(head_grads)
    got = got.astype(wide).reshape(kv_heads, share, rows, lanes).sum(axis=1)
    got = jnp.transpose(got, (1, 0, 2)).reshape(rows, 2, kv_heads // 2, lanes)
    cut = repeat * HEAD_DIM
    total = jnp.concatenate(
        [got[..., :cut].reshape(rows, 2, -1), got[..., cut:].reshape(rows, 2, -1)], axis=2
    )
    kept = pick(total, core, 1)
    given = pick(total, 1 - core, 1)
    front, back = net.ordered(kept, net.swap(given.astype(low)).astype(wide))
    grad_query, grad_key = front[:, :q_cols], front[:, q_cols:]
    grad_out, grad_value = back[:, :q_cols], back[:, q_cols:]

    def by_units(pieces):
        return jnp.transpose(pieces, (1, 0, 2)).reshape(rows, ranks * units).astype(wide)

    return (
        layer_output[None],
        input_grad[None],
        grad_query,
        grad_key,
        grad_value,
        grad_out,
        by_units(pair_grad[:, :, :units]),
        by_units(pair_grad[:, :, units:]),
        by_units(down_grad),
        gain_got[0],
        gain_got[1],
        gain_got[2],
        gain_got[3],
    )


def solution(mesh):
    tokens_spec = P("dp", "context", None)
    weight_spec = P(("dp", "context"), "tensor")
    gain_spec = P(("dp", "context"))
    return jax.shard_map(
        body,
        mesh=mesh,
        in_specs=(tokens_spec,) + (weight_spec,) * 7 + (gain_spec,) * 4 + (tokens_spec,),
        out_specs=(tokens_spec,) * 2 + (weight_spec,) * 7 + (gain_spec,) * 4,
        check_vma=False,
    )
```

```python
import jax
import jax.numpy as jnp
from jax import lax
from jax.experimental import pallas as pl
from jax.experimental.pallas import tpu as pltpu
from jax.sharding import PartitionSpec as P

HEAD_DIM = 256
LANES = 128
LANES = 128

epsilon = 1e-06
softcap = 50.0
theta = 10000.0
floor_value = -1e30
low = jnp.bfloat16
wide = jnp.float32
chip_axes = ("dp", "context")
all_axes = ("dp", "context", "tensor")


def product(left_side, right_side):
    return jnp.dot(left_side, right_side, preferred_element_type=wide)


def product_right_t(left_side, right_side):
    return lax.dot_general(left_side, right_side, (((1,), (1,)), ((), ())), preferred_element_type=wide)


def product_left_t(left_side, right_side):
    return lax.dot_general(left_side, right_side, (((0,), (0,)), ((), ())), preferred_element_type=wide)


def inverse_size(values):
    return lax.rsqrt(jnp.mean(values * values, axis=-1, keepdims=True) + epsilon)


def norm_back(unit, inverse, scaling, upstream):
    inner = upstream * scaling
    return inverse * (inner - unit * jnp.mean(inner * unit, axis=-1, keepdims=True))


def turn(values, cosine, sine_part):
    half_width = values.shape[-1] // 2
    former = values[..., :half_width]
    latter = values[..., half_width:]
    return jnp.concatenate(
        [former * cosine - latter * sine_part, latter * cosine + former * sine_part], axis=-1
    )


def geglu(gate_in, upward):
    return jax.nn.gelu(gate_in, approximate=True) * upward


def pick(array, at, axis):
    return lax.dynamic_index_in_dim(array, at, axis, keepdims=False)


def hold(*trees):
    return lax.optimization_barrier(trees)


def assembled(place, ranks, rows, upper, lower, others):
    count, units = len(others), others[0].shape[3]
    parts = upper.shape[3], lower.shape[3]

    def kernel(place_ref, upper_ref, lower_ref, *refs):
        out, own = refs[-1], place_ref[2]
        for at in range(count):
            begin = at * units
            out[0, own, 0, :, begin : begin + parts[0]] = upper_ref[0, at]
            out[0, own, 0, :, begin + parts[0] : begin + units] = lower_ref[0, at]
            for step in range(1, ranks):
                out[0, (own + step) % ranks, 0, :, begin : begin + units] = refs[at][0, step - 1]

    def around(line, side, place):
        return (line * 2 + (side ^ line), 0, 0, 0)

    def relative(line, side, place):
        return ((line ^ place[0]) * 2 + (side ^ place[1]), 0, 0, 0)

    whole = pl.pallas_call(
        kernel,
        grid_spec=pltpu.PrefetchScalarGridSpec(
            num_scalar_prefetch=1,
            grid=(2, 2),
            in_specs=[
                pl.BlockSpec((1, count, rows, parts[0]), relative),
                pl.BlockSpec((1, count, rows, parts[1]), relative),
            ]
            + [pl.BlockSpec((1, ranks - 1, rows, units), around)] * count,
            out_specs=pl.BlockSpec(
                (1, ranks, 1, rows, count * units), lambda line, side, place: (line, 0, side, 0, 0)
            ),
        ),
        out_shape=jax.ShapeDtypeStruct((2, ranks, 2, rows, count * units), low),
        compiler_params=pltpu.CompilerParams(vmem_limit_bytes=32 * 2**20),
        cost_estimate=pl.CostEstimate(
            flops=0, transcendentals=0, bytes_accessed=16 * ranks * rows * count * units
        ),
    )(place, upper, lower, *others)
    return whole.reshape(-1, count * units)


def by_part(place, whole, rows):
    ranks, some, lanes = whole.shape[2], whole.shape[3], whole.shape[4]

    def kernel(place_ref, whole_ref, *outs):
        for core in range(2):
            for step in range(ranks):
                outs[core][0, (place_ref[2] + step) % ranks, 0] = whole_ref[0, core, step, :rows]
        for step in range(ranks):
            outs[2][0, (place_ref[2] + step) % ranks, 0] = whole_ref[0, 0, step, rows:]

    def to(count):
        return pl.BlockSpec(
            (1, ranks, 1, count, lanes), lambda line, side, place: (line, 0, side, 0, 0)
        )

    front, back, after = pl.pallas_call(
        kernel,
        grid_spec=pltpu.PrefetchScalarGridSpec(
            num_scalar_prefetch=1,
            grid=(2, 2),
            in_specs=[
                pl.BlockSpec(
                    (1,) + whole.shape[1:],
                    lambda line, side, place: (line * 2 + (side ^ line), 0, 0, 0, 0),
                )
            ],
            out_specs=[to(rows), to(rows), to(some - rows)],
        ),
        out_shape=[
            jax.ShapeDtypeStruct((2, ranks, 2, count, lanes), low)
            for count in (rows, rows, some - rows)
        ],
        compiler_params=pltpu.CompilerParams(vmem_limit_bytes=32 * 2**20),
        cost_estimate=pl.CostEstimate(
            flops=0, transcendentals=0, bytes_accessed=32 * ranks * rows * lanes
        ),
    )(place, whole)
    return front.reshape(-1, lanes), back.reshape(-1, lanes), after


def side_by_side(pieces):
    ranks, rows, units = pieces.shape

    def kernel(in_ref, out):
        for rank in range(ranks):
            out[:, rank * units : (rank + 1) * units] = in_ref[rank].astype(wide)

    return pl.pallas_call(
        kernel,
        in_specs=[pl.BlockSpec(memory_space=pltpu.VMEM)],
        out_specs=pl.BlockSpec(memory_space=pltpu.VMEM),
        out_shape=jax.ShapeDtypeStruct((rows, ranks * units), wide),
        compiler_params=pltpu.CompilerParams(vmem_limit_bytes=32 * 2**20),
        cost_estimate=pl.CostEstimate(
            flops=0, transcendentals=0, bytes_accessed=6 * ranks * rows * units
        ),
    )(pieces)


class Slice:
    def __init__(self):
        self.dp = lax.axis_size("dp")
        self.context = lax.axis_size("context")
        self.ranks = self.context // 2
        self.chips = self.dp * self.context
        self.core = lax.axis_index("tensor")
        self.place = lax.axis_index("context")
        self.rank = self.place // 2
        self.side = self.place % 2
        self.line = lax.axis_index("dp")

    def send(self, block, where):
        pairs = []
        for dp in range(self.dp):
            for rank in range(self.ranks):
                for side in range(2):
                    pairs.append(
                        (self.index(dp, rank, side), self.index(*where(dp, rank, side)))
                    )
        return lax.ppermute(block, chip_axes, pairs)

    def index(self, dp, rank, side):
        return (dp * self.ranks + rank % self.ranks) * 2 + side

    def across(self, block):
        return self.send(block, lambda dp, rank, side: (dp, rank, 1 - side))

    def over(self, block):
        return self.send(block, lambda dp, rank, side: (1 - dp, rank, side))

    def along(self, block, step):
        if step % self.ranks == 0:
            return block
        return self.send(block, lambda dp, rank, side: (dp, rank + step, side))

    def swap(self, block):
        return lax.ppermute(block, "tensor", [(0, 1), (1, 0)])

    def ordered(self, mine, other):
        first = self.core == 0
        return jnp.where(first, mine, other), jnp.where(first, other, mine)

    def moves(self, block):
        return [self.along(block, step) for step in range(self.ranks)]

    def returned(self, blocks):
        total = 0.0
        for step, block in zip(range(0, self.ranks, self.ranks // len(blocks)), blocks, strict=True):
            if step:
                block = self.along(block.astype(low), -step)
            total = total + block.astype(wide)
        return total

    def to_ranks(self, array):
        if self.ranks != 4:
            return self.turned(self.exchanged(array), self.rank)
        own, after, far, before = [pick(array, (self.rank + step) % 4, 0) for step in range(4)]
        cut = far.shape[0] // 32 * 16
        back, ahead = self.along(far[:cut], -1), self.along(far[cut:], 2)
        from_before, from_after = self.along(after, 1), self.along(before, -1)
        back, ahead, from_before, from_after = hold(back, ahead, from_before, from_after)
        far = jnp.concatenate([self.along(back, -1), ahead])
        return jnp.stack([own, from_after, far, from_before])

    def exchanged(self, array):
        groups = [[rank * 2 + side for rank in range(self.ranks)] for side in range(2)]
        return lax.all_to_all(array, "context", 0, 0, tiled=True, axis_index_groups=groups)

    def turned(self, array, first):
        return lax.dynamic_slice_in_dim(jnp.concatenate([array, array]), first, array.shape[0], 0)

    def square(self):
        return [
            [self.index(dp, rank, side ^ dp) for dp in range(self.dp) for side in range(2)]
            for rank in range(self.ranks)
        ]

    def square_cores(self):
        return [[2 * chip + core for chip in chips for core in range(2)] for chips in self.square()]

    def heads_in(self, array):
        whole = lax.all_gather(
            array, all_axes, axis=0, tiled=False, axis_index_groups=self.square_cores()
        )
        return whole.reshape((4, 2) + array.shape)

    def heads_by_square(self, grads, rows):
        lanes = grads[0].shape[1]
        parts = [g.astype(low).reshape(self.dp, self.ranks, 2, rows, lanes) for g in grads]
        parts = [self.round_square(part) for part in parts]
        return jnp.stack(parts, axis=1).reshape(-1, lanes)

    def round_square(self, parts):
        return jnp.stack([parts[line, :, side ^ line] for line in range(2) for side in range(2)])

    def head_grads_out(self, parts, rows):
        total = lax.psum_scatter(
            parts,
            all_axes,
            scatter_dimension=0,
            tiled=True,
            axis_index_groups=self.square_cores(),
        )
        return total.reshape(self.ranks, rows, -1)

    def weights_in(self, array):
        ranks, rows, units = array.shape
        return lax.all_gather(array, chip_axes, axis=0, tiled=False, axis_index_groups=self.square())

    def by_model_row(self, whole):
        ranks = whole.shape[1]
        whole = self.turned(jnp.moveaxis(whole, 1, 0), ranks - self.rank)
        whole = jnp.stack(
            [whole[:, line * 2 + (side ^ line)] for line in range(2) for side in range(2)]
        ).reshape((2, 2, ranks) + whole.shape[2:])
        return jnp.transpose(whole, (0, 2, 1, 3, 4)).reshape(-1, whole.shape[-1])

    def by_square(self, grad, rows):
        parts = grad.astype(low).reshape(self.dp, self.ranks, 2, rows, -1)
        return self.round_square(parts).reshape(-1, grad.shape[1])

    def grads_out(self, parts, rows):
        total = lax.psum_scatter(
            parts, chip_axes, scatter_dimension=0, tiled=True, axis_index_groups=self.square()
        )
        return total.reshape(self.ranks, rows, -1)


def body(
    tokens,
    w_query,
    w_key,
    w_value,
    w_out,
    w_gate,
    w_up,
    w_down,
    gain_attn_in,
    gain_attn_out,
    gain_ffw_in,
    gain_ffw_out,
    cotangent,
):
    net = Slice()
    core, chips, ranks = net.core, net.chips, net.ranks
    span = tokens.shape[1]
    width = tokens.shape[2]
    half = span // 2
    rows = w_query.shape[0]
    heads = 2 * w_query.shape[1] // HEAD_DIM
    kv_heads = 2 * w_key.shape[1] // HEAD_DIM
    repeat = heads // kv_heads
    share = ranks // kv_heads
    score_scale = HEAD_DIM ** (-0.5)
    units = w_gate.shape[1] // ranks
    q_cols, k_cols = w_query.shape[1], w_key.shape[1]
    is_front = core == 0

    own_tokens = lax.dynamic_slice_in_dim(tokens[0], core * half, half, 0)
    upstream = lax.dynamic_slice_in_dim(cotangent[0], core * half, half, 0)

    front = jnp.concatenate([w_query, w_key], axis=1)
    back = jnp.concatenate([w_out, w_value], axis=1)
    mine = jnp.where(is_front, front, back)
    theirs = net.swap(jnp.where(is_front, back, front))
    low_heads, high_heads = net.ordered(mine, theirs)

    def by_group(begin, end):
        both = jnp.concatenate([low_heads[:, begin:end], high_heads[:, begin:end]], axis=1)
        return jnp.transpose(both.reshape(rows, kv_heads, -1), (1, 0, 2))

    lanes = (repeat + 1) * HEAD_DIM
    gain_row = jnp.concatenate([gain_attn_in, gain_attn_out, gain_ffw_in, gain_ffw_out])
    gain_row = jnp.pad(gain_row, (0, lanes - 4 * rows))
    head_sets = jnp.concatenate([by_group(0, q_cols), by_group(q_cols, q_cols + k_cols)], axis=2)
    head_sets = jnp.concatenate(
        [head_sets, jnp.broadcast_to(gain_row, (kv_heads, 1, lanes))], axis=1
    )
    part = net.to_ranks(jnp.repeat(head_sets, share, axis=0))

    def by_rank(w):
        return jnp.transpose(w.reshape(rows, ranks, units), (1, 0, 2))

    gate_set, up_set, down_set = by_rank(w_gate), by_rank(w_up), by_rank(w_down)
    token_blocks = jnp.stack(net.moves(own_tokens))

    own_inputs = own_tokens.astype(wide)
    block_places = (net.rank - jnp.arange(ranks)) % ranks * 2 * span
    offsets = jnp.arange(half, dtype=jnp.int32)
    line_places = (block_places[:, None] + offsets[None, :]).reshape(-1)
    places = line_places + net.side * span + core * half
    key_places = jnp.concatenate(
        [
            line_places + side * span + of * half
            for of in (core, 1 - core)
            for side in (net.side, 1 - net.side)
        ]
    )
    exponent = jnp.arange(HEAD_DIM // 2, dtype=wide) * (-2.0 / HEAD_DIM)
    angles = places.astype(wide)[:, None] * (theta**exponent)[None, :]
    cosine, sine_part = jnp.cos(angles), jnp.sin(angles)

    by_parts = rows % 16 == 0 and units % LANES == 0
    place = jnp.stack([net.line, net.side, net.rank]).astype(jnp.int32)
    if by_parts:
        own_units = jnp.stack(
            [lax.dynamic_slice_in_dim(w, net.rank * units, units, 1) for w in (w_gate, w_up, w_down)]
        )
        middle_lane = (units // LANES + 1) // 2 * LANES
        upper, lower = own_units[:, :, :middle_lane], own_units[:, :, middle_lane:]
        upper = jnp.stack([upper, net.across(upper)])
        lower = jnp.stack([lower, net.over(lower)])
        part, token_blocks, upper, lower, gate_set, up_set, down_set, cosine, sine_part = hold(
            part, token_blocks, upper, lower, gate_set, up_set, down_set, cosine, sine_part
        )
        upper = jnp.concatenate([upper, net.over(upper)])
        lower_side = net.across(lower)
        lower = jnp.stack([lower[0], lower_side[0], lower[1], lower_side[1]])
    else:
        part, token_blocks, gate_set, up_set, down_set = hold(
            part, token_blocks, gate_set, up_set, down_set
        )
    kept = 1 if by_parts else 0
    head_all = net.heads_in(part)
    gate_set = net.to_ranks(gate_set)
    gate_units = net.weights_in(gate_set[kept:])
    gate_set, up_set = hold(gate_set, up_set)
    up_set = net.to_ranks(up_set)
    up_units = net.weights_in(up_set[kept:])
    up_set, down_set = hold(up_set, down_set)
    down_set = net.to_ranks(down_set)
    down_units = net.weights_in(down_set[kept:])

    asked = tuple(range(0, ranks, share))

    def asked_rows(array):
        if share == 1:
            return array
        blocks = array.reshape((ranks, half) + array.shape[1:])
        return jnp.concatenate([blocks[step] for step in asked])

    def by_head(array):
        return jnp.concatenate(jnp.split(array, repeat, axis=1))

    def by_token(array):
        return jnp.concatenate(jnp.split(array, repeat), axis=1)

    cosine_heads = jnp.concatenate([asked_rows(cosine)] * repeat)
    sine_heads = jnp.concatenate([asked_rows(sine_part)] * repeat)
    head_cols = repeat * HEAD_DIM

    def attend(head_all, token_blocks):
        if by_parts:
            front_weights, back_weights, gain_rows = by_part(place, head_all, rows)
        else:
            front_weights, back_weights = [
                net.by_model_row(head_all[:, of, :, :rows]) for of in range(2)
            ]
            gain_rows = net.by_model_row(head_all[:, 0, :, rows:])
        gains = gain_rows.reshape(chips, lanes)[:, : 4 * rows].reshape(chips, 4, rows)
        gains = jnp.transpose(gains, (1, 0, 2)).reshape(4, width).astype(wide)
        inputs = token_blocks.reshape(-1, width).astype(wide)
        normed_low = (inputs * inverse_size(inputs) * gains[0]).astype(low)
        query_key = product(normed_low, front_weights)
        queries = turn(by_head(asked_rows(query_key[:, :head_cols])), cosine_heads, sine_heads)
        queries = queries.astype(low)
        keys = turn(query_key[:, head_cols:], cosine, sine_part).astype(low)
        values = product(normed_low, back_weights[:, head_cols:]).astype(low)
        own_kv = jnp.concatenate([keys, values], axis=1)
        side_kv = jnp.concatenate([own_kv, net.across(own_kv)])
        all_kv = jnp.concatenate([side_kv, net.swap(side_kv)])
        allowed = key_places[None, :] <= jnp.concatenate([asked_rows(places)] * repeat)[:, None]
        scores = product_right_t(queries, all_kv[:, :HEAD_DIM]) * score_scale
        bent = jnp.tanh(scores / softcap)
        capped = jnp.where(allowed, softcap * bent, floor_value)
        shifted = jnp.exp(capped - jnp.max(capped, axis=-1, keepdims=True))
        probabilities = shifted / jnp.sum(shifted, axis=-1, keepdims=True)
        mixed = product(probabilities.astype(low), all_kv[:, HEAD_DIM:])
        mixed_low = by_token(mixed.astype(low))
        out_parts = product_right_t(mixed_low, back_weights[:, :head_cols]).astype(low)
        return (
            front_weights,
            back_weights,
            gains,
            normed_low,
            queries,
            all_kv,
            probabilities,
            bent,
            mixed_low,
            out_parts,
        )

    (
        front_weights,
        back_weights,
        gains,
        normed_low,
        queries,
        all_kv,
        probabilities,
        bent,
        mixed_low,
        out_parts,
    ) = attend(head_all, token_blocks)
    scale_in, scale_mid, scale_pre, scale_out = gains[0], gains[1], gains[2], gains[3]
    w_out_head = back_weights[:, :head_cols]
    w_value_head = back_weights[:, head_cols:]
    all_keys, all_values = all_kv[:, :HEAD_DIM], all_kv[:, HEAD_DIM:]
    probabilities_low = probabilities.astype(low)
    inputs = token_blocks.reshape(-1, width).astype(wide)
    units_in = inputs * inverse_size(inputs)
    out_parts = out_parts.reshape(len(asked), half, width).astype(wide)
    projected = 0.0
    for at, step in enumerate(asked):
        block = out_parts[at]
        if step:
            block = net.along(block.astype(low), -step).astype(wide)
        projected = projected + block


    inverse_mid = inverse_size(projected)
    unit_mid = projected * inverse_mid
    middle = own_inputs + unit_mid * scale_mid
    inverse_pre = inverse_size(middle)
    unit_pre = middle * inverse_pre
    normed_two_low = (unit_pre * scale_pre).astype(low)
    two_blocks = jnp.stack(net.moves(normed_two_low)).reshape(-1, width)
    two_blocks, gate_units, up_units = hold(two_blocks, gate_units, up_units)
    if by_parts:
        pair_units = assembled(
            place, ranks, rows, upper[:, :2], lower[:, :2], [gate_units, up_units]
        )
    else:
        pair_units = jnp.concatenate(
            [net.by_model_row(gate_units), net.by_model_row(up_units)], axis=1
        )

    all_two = jnp.concatenate([two_blocks, net.swap(two_blocks)])
    pair = product(all_two, pair_units)
    gate_in, upward = pair[:, :units], pair[:, units:]
    hidden_low = geglu(gate_in, upward).astype(low)
    hidden_low, down_units = hold(hidden_low, down_units)
    if by_parts:
        down_units = assembled(place, ranks, rows, upper[:, 2:], lower[:, 2:], [down_units])
    else:
        down_units = net.by_model_row(down_units)

    def core_total(part):
        count = ranks * half
        part = part.astype(low)
        return part[:count].astype(wide) + net.swap(part[count:]).astype(wide)

    def line_total(own):
        return net.returned(list(own.reshape(ranks, half, width)))

    branch = line_total(core_total(product_right_t(hidden_low, down_units)))
    inverse_out = inverse_size(branch)
    unit_out = branch * inverse_out
    own_output = (middle + unit_out * scale_out).astype(low)

    grad_ffw_out = jnp.sum(upstream * unit_out, axis=0)
    d_branch_low = norm_back(unit_out, inverse_out, scale_out, upstream).astype(low)
    branch_blocks = jnp.stack(net.moves(d_branch_low)).reshape(-1, width)
    all_branch = jnp.concatenate([branch_blocks, net.swap(branch_blocks)])

    down_grad = net.by_square(product_left_t(all_branch, hidden_low), rows)
    down_grad, all_branch = hold(down_grad, all_branch)
    down_grad = net.grads_out(down_grad, rows)
    d_hidden = product(all_branch, down_units)
    _, pull = jax.vjp(geglu, gate_in, upward)
    d_gate, d_up = pull(d_hidden)
    d_gate_low, d_up_low = d_gate.astype(low), d_up.astype(low)
    d_two = product_right_t(jnp.concatenate([d_gate_low, d_up_low], axis=1), pair_units)
    d_two, d_gate_low, d_up_low, all_two = hold(
        core_total(d_two), d_gate_low, d_up_low, all_two
    )
    d_normed_two = line_total(d_two)
    gate_grad = net.by_square(product_left_t(all_two, d_gate_low), rows)
    up_grad = net.by_square(product_left_t(all_two, d_up_low), rows)
    d_normed_two, gate_grad, up_grad, down_grad = hold(
        d_normed_two, gate_grad, up_grad, down_grad
    )
    gate_grad = net.grads_out(gate_grad, rows)
    grad_ffw_in = jnp.sum(d_normed_two * unit_pre, axis=0)
    d_middle = upstream + norm_back(unit_pre, inverse_pre, scale_pre, d_normed_two)
    grad_attn_out = jnp.sum(d_middle * unit_mid, axis=0)
    d_projected_low = norm_back(unit_mid, inverse_mid, scale_mid, d_middle).astype(low)
    d_projected_low, up_grad = hold(d_projected_low, up_grad)
    up_grad = net.grads_out(up_grad, rows)
    d_projected_all = jnp.stack(net.moves(d_projected_low))
    d_projected_all, down_grad = hold(d_projected_all, down_grad)
    down_grad = net.exchanged(down_grad)
    d_projected_asked = asked_rows(d_projected_all.reshape(-1, width))
    d_mixed_low = by_head(product(d_projected_asked, w_out_head).astype(low))
    d_prob = product_right_t(d_mixed_low, all_values)
    delta = jnp.sum(probabilities * d_prob, axis=-1, keepdims=True)
    d_capped = probabilities * (d_prob - delta)
    d_scores = (d_capped * (1.0 - bent * bent)).astype(low)
    d_queries = product(d_scores, all_keys) * score_scale
    d_keys = product_left_t(d_scores, queries) * score_scale
    d_values = product_left_t(probabilities_low, d_mixed_low)
    count = all_keys.shape[0] // 2
    given = jnp.concatenate([d_keys[count:].astype(low), d_values[count:].astype(low)], axis=1)
    given = net.swap(given).astype(wide)
    d_keys = d_keys[:count] + given[:, :HEAD_DIM]
    d_values = d_values[:count] + given[:, HEAD_DIM:]
    count = count // 2
    given = jnp.concatenate([d_keys[count:].astype(low), d_values[count:].astype(low)], axis=1)
    given = net.across(given).astype(wide)
    d_keys = d_keys[:count] + given[:, :HEAD_DIM]
    d_values = d_values[:count] + given[:, HEAD_DIM:]
    d_query_low = by_token(turn(d_queries, cosine_heads, -sine_heads).astype(low))
    d_key_low = turn(d_keys, cosine, -sine_part).astype(low)
    if share != 1:
        blocks = jnp.zeros((ranks, half, repeat * HEAD_DIM), low)
        d_query_low = blocks.at[jnp.array(asked)].set(
            d_query_low.reshape(len(asked), half, repeat * HEAD_DIM)
        )
        d_query_low = d_query_low.reshape(-1, repeat * HEAD_DIM)
    d_value_low = d_values.astype(low)
    d_front_low = jnp.concatenate([d_query_low, d_key_low], axis=1)
    d_normed_part = product_right_t(d_front_low, front_weights)
    d_normed_part = d_normed_part + product_right_t(d_value_low, w_value_head)
    grad_attn_in = jnp.sum(d_normed_part * units_in, axis=0)
    d_normed_low = d_normed_part.astype(low).reshape(ranks, half, width)
    d_normed_low, d_front_low, d_value_low, down_grad, gate_grad = hold(
        d_normed_low, d_front_low, d_value_low, down_grad, gate_grad
    )
    gate_grad = net.exchanged(gate_grad)
    d_normed = net.returned(list(d_normed_low))
    front_grads = product_left_t(normed_low, d_front_low)
    back_grads = jnp.concatenate(
        [
            product_left_t(d_projected_asked, mixed_low),
            product_left_t(normed_low, d_value_low),
        ],
        axis=1,
    )
    head_grads = net.heads_by_square([front_grads, back_grads], rows)
    head_grads, gate_grad = hold(head_grads, gate_grad)
    head_grads = net.head_grads_out(head_grads, rows)
    up_grad, gate_grad = hold(up_grad, gate_grad)
    up_grad = net.exchanged(up_grad)
    up_grad, head_grads = hold(up_grad, head_grads)
    gain_grads = jnp.stack([grad_attn_in, grad_attn_out, grad_ffw_in, grad_ffw_out])
    gain_grads = gain_grads + net.swap(gain_grads)
    gain_grads = jnp.transpose(gain_grads.reshape(4, net.dp, ranks, 2, rows), (1, 2, 3, 0, 4))
    gain_grads = pick(gain_grads, net.line, 0) + net.over(pick(gain_grads, 1 - net.line, 0))
    gain_grads = pick(gain_grads, net.side, 1) + net.across(pick(gain_grads, 1 - net.side, 1))
    gain_got = pick(gain_grads, net.rank, 0)
    for step in range(1, ranks):
        gain_got = gain_got + net.along(pick(gain_grads, (net.rank + step) % ranks, 0), step)
    own_inverse = inverse_size(own_inputs)
    own_grad = d_middle + norm_back(own_inputs * own_inverse, own_inverse, scale_in, d_normed)
    layer_output = jnp.concatenate(net.ordered(own_output, net.swap(own_output)))
    input_grad = jnp.concatenate(net.ordered(own_grad, net.swap(own_grad)))
    got = net.exchanged(head_grads)
    got = got.astype(wide).reshape(kv_heads, share, rows, lanes).sum(axis=1)
    got = jnp.transpose(got, (1, 0, 2)).reshape(rows, 2, kv_heads // 2, lanes)
    cut = repeat * HEAD_DIM
    total = jnp.concatenate(
        [got[..., :cut].reshape(rows, 2, -1), got[..., cut:].reshape(rows, 2, -1)], axis=2
    )
    kept = pick(total, core, 1)
    given = pick(total, 1 - core, 1)
    front, back = net.ordered(kept, net.swap(given.astype(low)).astype(wide))
    grad_query, grad_key = front[:, :q_cols], front[:, q_cols:]
    grad_out, grad_value = back[:, :q_cols], back[:, q_cols:]

    def by_units(pieces):
        if by_parts:
            return side_by_side(pieces)
        return jnp.transpose(pieces, (1, 0, 2)).reshape(rows, ranks * units).astype(wide)

    return (
        layer_output[None],
        input_grad[None],
        grad_query,
        grad_key,
        grad_value,
        grad_out,
        by_units(gate_grad),
        by_units(up_grad),
        by_units(down_grad),
        gain_got[0],
        gain_got[1],
        gain_got[2],
        gain_got[3],
    )


def solution(mesh):
    tokens_spec = P("dp", "context", None)
    weight_spec = P(("dp", "context"), "tensor")
    gain_spec = P(("dp", "context"))
    return jax.shard_map(
        body,
        mesh=mesh,
        in_specs=(tokens_spec,) + (weight_spec,) * 7 + (gain_spec,) * 4 + (tokens_spec,),
        out_specs=(tokens_spec,) * 2 + (weight_spec,) * 7 + (gain_spec,) * 4,
        check_vma=False,
    )
```

```python
import jax
import jax.numpy as jnp
from jax import lax
from jax.experimental import pallas as pl
from jax.experimental.pallas import tpu as pltpu
from jax.sharding import PartitionSpec as P

HEAD_DIM = 256
LANES = 128
LANES = 128

epsilon = 1e-06
softcap = 50.0
theta = 10000.0
floor_value = -1e30
low = jnp.bfloat16
wide = jnp.float32
chip_axes = ("dp", "context")
all_axes = ("dp", "context", "tensor")


def product(left_side, right_side):
    return jnp.dot(left_side, right_side, preferred_element_type=wide)


def product_right_t(left_side, right_side):
    return lax.dot_general(left_side, right_side, (((1,), (1,)), ((), ())), preferred_element_type=wide)


def product_left_t(left_side, right_side):
    return lax.dot_general(left_side, right_side, (((0,), (0,)), ((), ())), preferred_element_type=wide)


def inverse_size(values):
    return lax.rsqrt(jnp.mean(values * values, axis=-1, keepdims=True) + epsilon)


def norm_back(unit, inverse, scaling, upstream):
    inner = upstream * scaling
    return inverse * (inner - unit * jnp.mean(inner * unit, axis=-1, keepdims=True))


def turn(values, cosine, sine_part):
    half_width = values.shape[-1] // 2
    former = values[..., :half_width]
    latter = values[..., half_width:]
    return jnp.concatenate(
        [former * cosine - latter * sine_part, latter * cosine + former * sine_part], axis=-1
    )


def geglu(gate_in, upward):
    return jax.nn.gelu(gate_in, approximate=True) * upward


def pick(array, at, axis):
    return lax.dynamic_index_in_dim(array, at, axis, keepdims=False)


def hold(*trees):
    return lax.optimization_barrier(trees)


def assembled(place, ranks, rows, upper, lower, others):
    count, units = len(others), others[0].shape[3]
    parts = upper.shape[3], lower.shape[3]

    def kernel(place_ref, upper_ref, lower_ref, *refs):
        out, own = refs[-1], place_ref[2]
        for at in range(count):
            begin = at * units
            out[0, own, 0, :, begin : begin + parts[0]] = upper_ref[0, at]
            out[0, own, 0, :, begin + parts[0] : begin + units] = lower_ref[0, at]
            for step in range(1, ranks):
                out[0, (own + step) % ranks, 0, :, begin : begin + units] = refs[at][0, step - 1]

    def around(line, side, place):
        return (line * 2 + (side ^ line), 0, 0, 0)

    def relative(line, side, place):
        return ((line ^ place[0]) * 2 + (side ^ place[1]), 0, 0, 0)

    whole = pl.pallas_call(
        kernel,
        grid_spec=pltpu.PrefetchScalarGridSpec(
            num_scalar_prefetch=1,
            grid=(2, 2),
            in_specs=[
                pl.BlockSpec((1, count, rows, parts[0]), relative),
                pl.BlockSpec((1, count, rows, parts[1]), relative),
            ]
            + [pl.BlockSpec((1, ranks - 1, rows, units), around)] * count,
            out_specs=pl.BlockSpec(
                (1, ranks, 1, rows, count * units), lambda line, side, place: (line, 0, side, 0, 0)
            ),
        ),
        out_shape=jax.ShapeDtypeStruct((2, ranks, 2, rows, count * units), low),
        compiler_params=pltpu.CompilerParams(vmem_limit_bytes=32 * 2**20),
        cost_estimate=pl.CostEstimate(
            flops=0, transcendentals=0, bytes_accessed=16 * ranks * rows * count * units
        ),
    )(place, upper, lower, *others)
    return whole.reshape(-1, count * units)


def by_part(place, whole, rows):
    ranks, some, lanes = whole.shape[2], whole.shape[3], whole.shape[4]

    def kernel(place_ref, whole_ref, *outs):
        for core in range(2):
            for step in range(ranks):
                outs[core][0, (place_ref[2] + step) % ranks, 0] = whole_ref[0, core, step, :rows]
        for step in range(ranks):
            outs[2][0, (place_ref[2] + step) % ranks, 0] = whole_ref[0, 0, step, rows:]

    def to(count):
        return pl.BlockSpec(
            (1, ranks, 1, count, lanes), lambda line, side, place: (line, 0, side, 0, 0)
        )

    front, back, after = pl.pallas_call(
        kernel,
        grid_spec=pltpu.PrefetchScalarGridSpec(
            num_scalar_prefetch=1,
            grid=(2, 2),
            in_specs=[
                pl.BlockSpec(
                    (1,) + whole.shape[1:],
                    lambda line, side, place: (line * 2 + (side ^ line), 0, 0, 0, 0),
                )
            ],
            out_specs=[to(rows), to(rows), to(some - rows)],
        ),
        out_shape=[
            jax.ShapeDtypeStruct((2, ranks, 2, count, lanes), low)
            for count in (rows, rows, some - rows)
        ],
        compiler_params=pltpu.CompilerParams(vmem_limit_bytes=32 * 2**20),
        cost_estimate=pl.CostEstimate(
            flops=0, transcendentals=0, bytes_accessed=32 * ranks * rows * lanes
        ),
    )(place, whole)
    return front.reshape(-1, lanes), back.reshape(-1, lanes), after


def side_by_side(pieces):
    ranks, rows, units = pieces.shape

    def kernel(in_ref, out):
        for rank in range(ranks):
            out[:, rank * units : (rank + 1) * units] = in_ref[rank].astype(wide)

    return pl.pallas_call(
        kernel,
        in_specs=[pl.BlockSpec(memory_space=pltpu.VMEM)],
        out_specs=pl.BlockSpec(memory_space=pltpu.VMEM),
        out_shape=jax.ShapeDtypeStruct((rows, ranks * units), wide),
        compiler_params=pltpu.CompilerParams(vmem_limit_bytes=32 * 2**20),
        cost_estimate=pl.CostEstimate(
            flops=0, transcendentals=0, bytes_accessed=6 * ranks * rows * units
        ),
    )(pieces)


class Slice:
    def __init__(self):
        self.dp = lax.axis_size("dp")
        self.context = lax.axis_size("context")
        self.ranks = self.context // 2
        self.chips = self.dp * self.context
        self.core = lax.axis_index("tensor")
        self.place = lax.axis_index("context")
        self.rank = self.place // 2
        self.side = self.place % 2
        self.line = lax.axis_index("dp")

    def send(self, block, where):
        pairs = []
        for dp in range(self.dp):
            for rank in range(self.ranks):
                for side in range(2):
                    pairs.append(
                        (self.index(dp, rank, side), self.index(*where(dp, rank, side)))
                    )
        return lax.ppermute(block, chip_axes, pairs)

    def index(self, dp, rank, side):
        return (dp * self.ranks + rank % self.ranks) * 2 + side

    def across(self, block):
        return self.send(block, lambda dp, rank, side: (dp, rank, 1 - side))

    def over(self, block):
        return self.send(block, lambda dp, rank, side: (1 - dp, rank, side))

    def along(self, block, step):
        if step % self.ranks == 0:
            return block
        return self.send(block, lambda dp, rank, side: (dp, rank + step, side))

    def swap(self, block):
        return lax.ppermute(block, "tensor", [(0, 1), (1, 0)])

    def ordered(self, mine, other):
        first = self.core == 0
        return jnp.where(first, mine, other), jnp.where(first, other, mine)

    def moves(self, block):
        return [self.along(block, step) for step in range(self.ranks)]

    def returned(self, blocks):
        total = 0.0
        for step, block in zip(range(0, self.ranks, self.ranks // len(blocks)), blocks, strict=True):
            if step:
                block = self.along(block.astype(low), -step)
            total = total + block.astype(wide)
        return total

    def to_ranks(self, array):
        pieces = [self.along(pick(array, (self.rank - step) % self.ranks, 0), -step) for step in range(self.ranks)]
        return jnp.stack(pieces)

    def exchanged(self, array):
        groups = [[rank * 2 + side for rank in range(self.ranks)] for side in range(2)]
        return lax.all_to_all(array, "context", 0, 0, tiled=True, axis_index_groups=groups)

    def turned(self, array, first):
        return lax.dynamic_slice_in_dim(jnp.concatenate([array, array]), first, array.shape[0], 0)

    def square(self):
        return [
            [self.index(dp, rank, side ^ dp) for dp in range(self.dp) for side in range(2)]
            for rank in range(self.ranks)
        ]

    def square_cores(self):
        return [[2 * chip + core for chip in chips for core in range(2)] for chips in self.square()]

    def heads_in(self, array):
        whole = lax.all_gather(
            array, all_axes, axis=0, tiled=False, axis_index_groups=self.square_cores()
        )
        return whole.reshape((4, 2) + array.shape)

    def heads_by_square(self, grads, rows):
        lanes = grads[0].shape[1]
        parts = [g.astype(low).reshape(self.dp, self.ranks, 2, rows, lanes) for g in grads]
        parts = [self.round_square(part) for part in parts]
        return jnp.stack(parts, axis=1).reshape(-1, lanes)

    def round_square(self, parts):
        return jnp.stack([parts[line, :, side ^ line] for line in range(2) for side in range(2)])

    def head_grads_out(self, parts, rows):
        total = lax.psum_scatter(
            parts,
            all_axes,
            scatter_dimension=0,
            tiled=True,
            axis_index_groups=self.square_cores(),
        )
        return total.reshape(self.ranks, rows, -1)

    def weights_in(self, array):
        ranks, rows, units = array.shape
        return lax.all_gather(array, chip_axes, axis=0, tiled=False, axis_index_groups=self.square())

    def by_model_row(self, whole):
        ranks = whole.shape[1]
        whole = self.turned(jnp.moveaxis(whole, 1, 0), ranks - self.rank)
        whole = jnp.stack(
            [whole[:, line * 2 + (side ^ line)] for line in range(2) for side in range(2)]
        ).reshape((2, 2, ranks) + whole.shape[2:])
        return jnp.transpose(whole, (0, 2, 1, 3, 4)).reshape(-1, whole.shape[-1])

    def by_square(self, grad, rows):
        parts = grad.astype(low).reshape(self.dp, self.ranks, 2, rows, -1)
        return self.round_square(parts).reshape(-1, grad.shape[1])

    def grads_out(self, parts, rows):
        total = lax.psum_scatter(
            parts, chip_axes, scatter_dimension=0, tiled=True, axis_index_groups=self.square()
        )
        return total.reshape(self.ranks, rows, -1)


def body(
    tokens,
    w_query,
    w_key,
    w_value,
    w_out,
    w_gate,
    w_up,
    w_down,
    gain_attn_in,
    gain_attn_out,
    gain_ffw_in,
    gain_ffw_out,
    cotangent,
):
    net = Slice()
    core, chips, ranks = net.core, net.chips, net.ranks
    span = tokens.shape[1]
    width = tokens.shape[2]
    half = span // 2
    rows = w_query.shape[0]
    heads = 2 * w_query.shape[1] // HEAD_DIM
    kv_heads = 2 * w_key.shape[1] // HEAD_DIM
    repeat = heads // kv_heads
    share = ranks // kv_heads
    score_scale = HEAD_DIM ** (-0.5)
    units = w_gate.shape[1] // ranks
    q_cols, k_cols = w_query.shape[1], w_key.shape[1]
    is_front = core == 0

    own_tokens = lax.dynamic_slice_in_dim(tokens[0], core * half, half, 0)
    upstream = lax.dynamic_slice_in_dim(cotangent[0], core * half, half, 0)

    front = jnp.concatenate([w_query, w_key], axis=1)
    back = jnp.concatenate([w_out, w_value], axis=1)
    mine = jnp.where(is_front, front, back)
    theirs = net.swap(jnp.where(is_front, back, front))
    low_heads, high_heads = net.ordered(mine, theirs)

    def by_group(begin, end):
        both = jnp.concatenate([low_heads[:, begin:end], high_heads[:, begin:end]], axis=1)
        return jnp.transpose(both.reshape(rows, kv_heads, -1), (1, 0, 2))

    lanes = (repeat + 1) * HEAD_DIM
    gain_row = jnp.concatenate([gain_attn_in, gain_attn_out, gain_ffw_in, gain_ffw_out])
    gain_row = jnp.pad(gain_row, (0, lanes - 4 * rows))
    head_sets = jnp.concatenate([by_group(0, q_cols), by_group(q_cols, q_cols + k_cols)], axis=2)
    head_sets = jnp.concatenate(
        [head_sets, jnp.broadcast_to(gain_row, (kv_heads, 1, lanes))], axis=1
    )
    part = net.to_ranks(jnp.repeat(head_sets, share, axis=0))

    def by_rank(w):
        return jnp.transpose(w.reshape(rows, ranks, units), (1, 0, 2))

    gate_set, up_set, down_set = by_rank(w_gate), by_rank(w_up), by_rank(w_down)
    token_blocks = jnp.stack(net.moves(own_tokens))

    own_inputs = own_tokens.astype(wide)
    block_places = (net.rank - jnp.arange(ranks)) % ranks * 2 * span
    offsets = jnp.arange(half, dtype=jnp.int32)
    line_places = (block_places[:, None] + offsets[None, :]).reshape(-1)
    places = line_places + net.side * span + core * half
    key_places = jnp.concatenate(
        [
            line_places + side * span + of * half
            for of in (core, 1 - core)
            for side in (net.side, 1 - net.side)
        ]
    )
    exponent = jnp.arange(HEAD_DIM // 2, dtype=wide) * (-2.0 / HEAD_DIM)
    angles = places.astype(wide)[:, None] * (theta**exponent)[None, :]
    cosine, sine_part = jnp.cos(angles), jnp.sin(angles)

    by_parts = rows % 16 == 0 and units % LANES == 0
    place = jnp.stack([net.line, net.side, net.rank]).astype(jnp.int32)
    if by_parts:
        own_units = jnp.stack(
            [lax.dynamic_slice_in_dim(w, net.rank * units, units, 1) for w in (w_gate, w_up, w_down)]
        )
        middle_lane = (units // LANES + 1) // 2 * LANES
        upper, lower = own_units[:, :, :middle_lane], own_units[:, :, middle_lane:]
        upper = jnp.stack([upper, net.across(upper)])
        lower = jnp.stack([lower, net.over(lower)])
        part, token_blocks, upper, lower, gate_set, up_set, down_set, cosine, sine_part = hold(
            part, token_blocks, upper, lower, gate_set, up_set, down_set, cosine, sine_part
        )
        upper = jnp.concatenate([upper, net.over(upper)])
        lower_side = net.across(lower)
        lower = jnp.stack([lower[0], lower_side[0], lower[1], lower_side[1]])
    else:
        part, token_blocks, gate_set, up_set, down_set = hold(
            part, token_blocks, gate_set, up_set, down_set
        )
    kept = 1 if by_parts else 0
    head_all = net.heads_in(part)
    gate_set = net.to_ranks(gate_set)
    gate_units = net.weights_in(gate_set[kept:])
    gate_set, up_set = hold(gate_set, up_set)
    up_set = net.to_ranks(up_set)
    up_units = net.weights_in(up_set[kept:])
    up_set, down_set = hold(up_set, down_set)
    down_set = net.to_ranks(down_set)
    down_units = net.weights_in(down_set[kept:])

    asked = tuple(range(0, ranks, share))

    def asked_rows(array):
        if share == 1:
            return array
        blocks = array.reshape((ranks, half) + array.shape[1:])
        return jnp.concatenate([blocks[step] for step in asked])

    def by_head(array):
        return jnp.concatenate(jnp.split(array, repeat, axis=1))

    def by_token(array):
        return jnp.concatenate(jnp.split(array, repeat), axis=1)

    cosine_heads = jnp.concatenate([asked_rows(cosine)] * repeat)
    sine_heads = jnp.concatenate([asked_rows(sine_part)] * repeat)
    head_cols = repeat * HEAD_DIM

    def attend(head_all, token_blocks):
        if by_parts:
            front_weights, back_weights, gain_rows = by_part(place, head_all, rows)
        else:
            front_weights, back_weights = [
                net.by_model_row(head_all[:, of, :, :rows]) for of in range(2)
            ]
            gain_rows = net.by_model_row(head_all[:, 0, :, rows:])
        gains = gain_rows.reshape(chips, lanes)[:, : 4 * rows].reshape(chips, 4, rows)
        gains = jnp.transpose(gains, (1, 0, 2)).reshape(4, width).astype(wide)
        inputs = token_blocks.reshape(-1, width).astype(wide)
        normed_low = (inputs * inverse_size(inputs) * gains[0]).astype(low)
        keys = turn(product(normed_low, front_weights[:, head_cols:]), cosine, sine_part).astype(low)
        values = product(normed_low, back_weights[:, head_cols:]).astype(low)
        own_kv = jnp.concatenate([keys, values], axis=1)
        side_kv = jnp.concatenate([own_kv, net.across(own_kv)])
        all_kv = jnp.concatenate([side_kv, net.swap(side_kv)])
        queries = product(asked_rows(normed_low), front_weights[:, :head_cols])
        queries = turn(by_head(queries), cosine_heads, sine_heads).astype(low)
        allowed = key_places[None, :] <= jnp.concatenate([asked_rows(places)] * repeat)[:, None]
        scores = product_right_t(queries, all_kv[:, :HEAD_DIM]) * score_scale
        bent = jnp.tanh(scores / softcap)
        capped = jnp.where(allowed, softcap * bent, floor_value)
        shifted = jnp.exp(capped - jnp.max(capped, axis=-1, keepdims=True))
        probabilities = shifted / jnp.sum(shifted, axis=-1, keepdims=True)
        mixed = product(probabilities.astype(low), all_kv[:, HEAD_DIM:])
        mixed_low = by_token(mixed.astype(low))
        out_parts = product_right_t(mixed_low, back_weights[:, :head_cols]).astype(low)
        return (
            front_weights,
            back_weights,
            gains,
            normed_low,
            queries,
            all_kv,
            probabilities,
            bent,
            mixed_low,
            out_parts,
        )

    (
        front_weights,
        back_weights,
        gains,
        normed_low,
        queries,
        all_kv,
        probabilities,
        bent,
        mixed_low,
        out_parts,
    ) = attend(head_all, token_blocks)
    scale_in, scale_mid, scale_pre, scale_out = gains[0], gains[1], gains[2], gains[3]
    w_out_head = back_weights[:, :head_cols]
    w_value_head = back_weights[:, head_cols:]
    all_keys, all_values = all_kv[:, :HEAD_DIM], all_kv[:, HEAD_DIM:]
    probabilities_low = probabilities.astype(low)
    inputs = token_blocks.reshape(-1, width).astype(wide)
    units_in = inputs * inverse_size(inputs)
    out_parts = out_parts.reshape(len(asked), half, width).astype(wide)
    projected = 0.0
    for at, step in enumerate(asked):
        block = out_parts[at]
        if step:
            block = net.along(block.astype(low), -step).astype(wide)
        projected = projected + block


    inverse_mid = inverse_size(projected)
    unit_mid = projected * inverse_mid
    middle = own_inputs + unit_mid * scale_mid
    inverse_pre = inverse_size(middle)
    unit_pre = middle * inverse_pre
    normed_two_low = (unit_pre * scale_pre).astype(low)
    two_blocks = jnp.stack(net.moves(normed_two_low)).reshape(-1, width)
    two_blocks, gate_units, up_units = hold(two_blocks, gate_units, up_units)
    if by_parts:
        pair_units = assembled(
            place, ranks, rows, upper[:, :2], lower[:, :2], [gate_units, up_units]
        )
    else:
        pair_units = jnp.concatenate(
            [net.by_model_row(gate_units), net.by_model_row(up_units)], axis=1
        )

    all_two = jnp.concatenate([two_blocks, net.swap(two_blocks)])
    pair = product(all_two, pair_units)
    gate_in, upward = pair[:, :units], pair[:, units:]
    hidden_low = geglu(gate_in, upward).astype(low)
    hidden_low, down_units = hold(hidden_low, down_units)
    if by_parts:
        down_units = assembled(place, ranks, rows, upper[:, 2:], lower[:, 2:], [down_units])
    else:
        down_units = net.by_model_row(down_units)

    def core_total(part):
        count = ranks * half
        part = part.astype(low)
        return part[:count].astype(wide) + net.swap(part[count:]).astype(wide)

    def line_total(own):
        return net.returned(list(own.reshape(ranks, half, width)))

    branch = line_total(core_total(product_right_t(hidden_low, down_units)))
    inverse_out = inverse_size(branch)
    unit_out = branch * inverse_out
    own_output = (middle + unit_out * scale_out).astype(low)

    grad_ffw_out = jnp.sum(upstream * unit_out, axis=0)
    d_branch_low = norm_back(unit_out, inverse_out, scale_out, upstream).astype(low)
    branch_blocks = jnp.stack(net.moves(d_branch_low)).reshape(-1, width)
    all_branch = jnp.concatenate([branch_blocks, net.swap(branch_blocks)])

    down_grad = net.by_square(product_left_t(all_branch, hidden_low), rows)
    down_grad, all_branch = hold(down_grad, all_branch)
    down_grad = net.grads_out(down_grad, rows)
    d_hidden = product(all_branch, down_units)
    _, pull = jax.vjp(geglu, gate_in, upward)
    d_gate, d_up = pull(d_hidden)
    d_gate_low, d_up_low = d_gate.astype(low), d_up.astype(low)
    d_two = product_right_t(jnp.concatenate([d_gate_low, d_up_low], axis=1), pair_units)
    d_two, d_gate_low, d_up_low, all_two = hold(
        core_total(d_two), d_gate_low, d_up_low, all_two
    )
    d_normed_two = line_total(d_two)
    gate_grad = net.by_square(product_left_t(all_two, d_gate_low), rows)
    up_grad = net.by_square(product_left_t(all_two, d_up_low), rows)
    d_normed_two, gate_grad, up_grad, down_grad = hold(
        d_normed_two, gate_grad, up_grad, down_grad
    )
    gate_grad = net.grads_out(gate_grad, rows)
    grad_ffw_in = jnp.sum(d_normed_two * unit_pre, axis=0)
    d_middle = upstream + norm_back(unit_pre, inverse_pre, scale_pre, d_normed_two)
    grad_attn_out = jnp.sum(d_middle * unit_mid, axis=0)
    d_projected_low = norm_back(unit_mid, inverse_mid, scale_mid, d_middle).astype(low)
    d_projected_low, up_grad = hold(d_projected_low, up_grad)
    up_grad = net.grads_out(up_grad, rows)
    d_projected_all = jnp.stack(net.moves(d_projected_low))
    d_projected_all, down_grad = hold(d_projected_all, down_grad)
    down_grad = net.exchanged(down_grad)
    d_projected_asked = asked_rows(d_projected_all.reshape(-1, width))
    d_mixed_low = by_head(product(d_projected_asked, w_out_head).astype(low))
    d_prob = product_right_t(d_mixed_low, all_values)
    delta = jnp.sum(probabilities * d_prob, axis=-1, keepdims=True)
    d_capped = probabilities * (d_prob - delta)
    d_scores = (d_capped * (1.0 - bent * bent)).astype(low)
    d_queries = product(d_scores, all_keys) * score_scale
    d_keys = product_left_t(d_scores, queries) * score_scale
    d_values = product_left_t(probabilities_low, d_mixed_low)
    count = all_keys.shape[0] // 2
    given = jnp.concatenate([d_keys[count:].astype(low), d_values[count:].astype(low)], axis=1)
    given = net.swap(given).astype(wide)
    d_keys = d_keys[:count] + given[:, :HEAD_DIM]
    d_values = d_values[:count] + given[:, HEAD_DIM:]
    count = count // 2
    given = jnp.concatenate([d_keys[count:].astype(low), d_values[count:].astype(low)], axis=1)
    given = net.across(given).astype(wide)
    d_keys = d_keys[:count] + given[:, :HEAD_DIM]
    d_values = d_values[:count] + given[:, HEAD_DIM:]
    d_query_low = by_token(turn(d_queries, cosine_heads, -sine_heads).astype(low))
    d_key_low = turn(d_keys, cosine, -sine_part).astype(low)
    if share != 1:
        blocks = jnp.zeros((ranks, half, repeat * HEAD_DIM), low)
        d_query_low = blocks.at[jnp.array(asked)].set(
            d_query_low.reshape(len(asked), half, repeat * HEAD_DIM)
        )
        d_query_low = d_query_low.reshape(-1, repeat * HEAD_DIM)
    d_value_low = d_values.astype(low)
    d_front_low = jnp.concatenate([d_query_low, d_key_low], axis=1)
    d_normed_part = product_right_t(d_front_low, front_weights)
    d_normed_part = d_normed_part + product_right_t(d_value_low, w_value_head)
    grad_attn_in = jnp.sum(d_normed_part * units_in, axis=0)
    d_normed_low = d_normed_part.astype(low).reshape(ranks, half, width)
    d_normed_low, d_front_low, d_value_low, down_grad, gate_grad = hold(
        d_normed_low, d_front_low, d_value_low, down_grad, gate_grad
    )
    gate_grad = net.exchanged(gate_grad)
    d_normed = net.returned(list(d_normed_low))
    front_grads = product_left_t(normed_low, d_front_low)
    back_grads = jnp.concatenate(
        [
            product_left_t(d_projected_asked, mixed_low),
            product_left_t(normed_low, d_value_low),
        ],
        axis=1,
    )
    head_grads = net.heads_by_square([front_grads, back_grads], rows)
    head_grads, gate_grad = hold(head_grads, gate_grad)
    head_grads = net.head_grads_out(head_grads, rows)
    up_grad, gate_grad = hold(up_grad, gate_grad)
    up_grad = net.exchanged(up_grad)
    up_grad, head_grads = hold(up_grad, head_grads)
    gain_grads = jnp.stack([grad_attn_in, grad_attn_out, grad_ffw_in, grad_ffw_out])
    gain_grads = gain_grads + net.swap(gain_grads)
    gain_grads = jnp.transpose(gain_grads.reshape(4, net.dp, ranks, 2, rows), (1, 2, 3, 0, 4))
    gain_grads = pick(gain_grads, net.line, 0) + net.over(pick(gain_grads, 1 - net.line, 0))
    gain_grads = pick(gain_grads, net.side, 1) + net.across(pick(gain_grads, 1 - net.side, 1))
    gain_got = pick(gain_grads, net.rank, 0)
    for step in range(1, ranks):
        gain_got = gain_got + net.along(pick(gain_grads, (net.rank + step) % ranks, 0), step)
    own_inverse = inverse_size(own_inputs)
    own_grad = d_middle + norm_back(own_inputs * own_inverse, own_inverse, scale_in, d_normed)
    layer_output = jnp.concatenate(net.ordered(own_output, net.swap(own_output)))
    input_grad = jnp.concatenate(net.ordered(own_grad, net.swap(own_grad)))
    got = net.exchanged(head_grads)
    got = got.astype(wide).reshape(kv_heads, share, rows, lanes).sum(axis=1)
    got = jnp.transpose(got, (1, 0, 2)).reshape(rows, 2, kv_heads // 2, lanes)
    cut = repeat * HEAD_DIM
    total = jnp.concatenate(
        [got[..., :cut].reshape(rows, 2, -1), got[..., cut:].reshape(rows, 2, -1)], axis=2
    )
    kept = pick(total, core, 1)
    given = pick(total, 1 - core, 1)
    front, back = net.ordered(kept, net.swap(given.astype(low)).astype(wide))
    grad_query, grad_key = front[:, :q_cols], front[:, q_cols:]
    grad_out, grad_value = back[:, :q_cols], back[:, q_cols:]

    def by_units(pieces):
        if by_parts:
            return side_by_side(pieces)
        return jnp.transpose(pieces, (1, 0, 2)).reshape(rows, ranks * units).astype(wide)

    return (
        layer_output[None],
        input_grad[None],
        grad_query,
        grad_key,
        grad_value,
        grad_out,
        by_units(gate_grad),
        by_units(up_grad),
        by_units(down_grad),
        gain_got[0],
        gain_got[1],
        gain_got[2],
        gain_got[3],
    )


def solution(mesh):
    tokens_spec = P("dp", "context", None)
    weight_spec = P(("dp", "context"), "tensor")
    gain_spec = P(("dp", "context"))
    return jax.shard_map(
        body,
        mesh=mesh,
        in_specs=(tokens_spec,) + (weight_spec,) * 7 + (gain_spec,) * 4 + (tokens_spec,),
        out_specs=(tokens_spec,) * 2 + (weight_spec,) * 7 + (gain_spec,) * 4,
        check_vma=False,
    )
```

```python
import jax
import jax.numpy as jnp
from jax import lax
from jax.experimental import pallas as pl
from jax.experimental.pallas import tpu as pltpu
from jax.sharding import PartitionSpec as P

HEAD_DIM = 256
LANES = 128
LANES = 128

epsilon = 1e-06
softcap = 50.0
theta = 10000.0
floor_value = -1e30
low = jnp.bfloat16
wide = jnp.float32
chip_axes = ("dp", "context")
all_axes = ("dp", "context", "tensor")


def product(left_side, right_side):
    return jnp.dot(left_side, right_side, preferred_element_type=wide)


def product_right_t(left_side, right_side):
    return lax.dot_general(left_side, right_side, (((1,), (1,)), ((), ())), preferred_element_type=wide)


def product_left_t(left_side, right_side):
    return lax.dot_general(left_side, right_side, (((0,), (0,)), ((), ())), preferred_element_type=wide)


def inverse_size(values):
    return lax.rsqrt(jnp.mean(values * values, axis=-1, keepdims=True) + epsilon)


def norm_back(unit, inverse, scaling, upstream):
    inner = upstream * scaling
    return inverse * (inner - unit * jnp.mean(inner * unit, axis=-1, keepdims=True))


def turn(values, cosine, sine_part):
    half_width = values.shape[-1] // 2
    former = values[..., :half_width]
    latter = values[..., half_width:]
    return jnp.concatenate(
        [former * cosine - latter * sine_part, latter * cosine + former * sine_part], axis=-1
    )


def geglu(gate_in, upward):
    return jax.nn.gelu(gate_in, approximate=True) * upward


def pick(array, at, axis):
    return lax.dynamic_index_in_dim(array, at, axis, keepdims=False)


def hold(*trees):
    return lax.optimization_barrier(trees)


def assembled(place, ranks, rows, upper, lower, others):
    count, units = len(others), others[0].shape[3]
    parts = upper.shape[3], lower.shape[3]

    def kernel(place_ref, upper_ref, lower_ref, *refs):
        out, own = refs[-1], place_ref[2]
        for at in range(count):
            begin = at * units
            out[0, own, 0, :, begin : begin + parts[0]] = upper_ref[0, at]
            out[0, own, 0, :, begin + parts[0] : begin + units] = lower_ref[0, at]
            for step in range(1, ranks):
                out[0, (own + step) % ranks, 0, :, begin : begin + units] = refs[at][0, step - 1]

    def around(line, side, place):
        return (line * 2 + (side ^ line), 0, 0, 0)

    def relative(line, side, place):
        return ((line ^ place[0]) * 2 + (side ^ place[1]), 0, 0, 0)

    whole = pl.pallas_call(
        kernel,
        grid_spec=pltpu.PrefetchScalarGridSpec(
            num_scalar_prefetch=1,
            grid=(2, 2),
            in_specs=[
                pl.BlockSpec((1, count, rows, parts[0]), relative),
                pl.BlockSpec((1, count, rows, parts[1]), relative),
            ]
            + [pl.BlockSpec((1, ranks - 1, rows, units), around)] * count,
            out_specs=pl.BlockSpec(
                (1, ranks, 1, rows, count * units), lambda line, side, place: (line, 0, side, 0, 0)
            ),
        ),
        out_shape=jax.ShapeDtypeStruct((2, ranks, 2, rows, count * units), low),
        compiler_params=pltpu.CompilerParams(vmem_limit_bytes=32 * 2**20),
        cost_estimate=pl.CostEstimate(
            flops=0, transcendentals=0, bytes_accessed=16 * ranks * rows * count * units
        ),
    )(place, upper, lower, *others)
    return whole.reshape(-1, count * units)


def by_part(place, whole, rows):
    ranks, some, lanes = whole.shape[2], whole.shape[3], whole.shape[4]

    def kernel(place_ref, whole_ref, *outs):
        for core in range(2):
            for step in range(ranks):
                outs[core][0, (place_ref[2] + step) % ranks, 0] = whole_ref[0, core, step, :rows]
        for step in range(ranks):
            outs[2][0, (place_ref[2] + step) % ranks, 0] = whole_ref[0, 0, step, rows:]

    def to(count):
        return pl.BlockSpec(
            (1, ranks, 1, count, lanes), lambda line, side, place: (line, 0, side, 0, 0)
        )

    front, back, after = pl.pallas_call(
        kernel,
        grid_spec=pltpu.PrefetchScalarGridSpec(
            num_scalar_prefetch=1,
            grid=(2, 2),
            in_specs=[
                pl.BlockSpec(
                    (1,) + whole.shape[1:],
                    lambda line, side, place: (line * 2 + (side ^ line), 0, 0, 0, 0),
                )
            ],
            out_specs=[to(rows), to(rows), to(some - rows)],
        ),
        out_shape=[
            jax.ShapeDtypeStruct((2, ranks, 2, count, lanes), low)
            for count in (rows, rows, some - rows)
        ],
        compiler_params=pltpu.CompilerParams(vmem_limit_bytes=32 * 2**20),
        cost_estimate=pl.CostEstimate(
            flops=0, transcendentals=0, bytes_accessed=32 * ranks * rows * lanes
        ),
    )(place, whole)
    return front.reshape(-1, lanes), back.reshape(-1, lanes), after


def side_by_side(pieces):
    ranks, rows, units = pieces.shape

    def kernel(in_ref, out):
        for rank in range(ranks):
            out[:, rank * units : (rank + 1) * units] = in_ref[rank].astype(wide)

    return pl.pallas_call(
        kernel,
        in_specs=[pl.BlockSpec(memory_space=pltpu.VMEM)],
        out_specs=pl.BlockSpec(memory_space=pltpu.VMEM),
        out_shape=jax.ShapeDtypeStruct((rows, ranks * units), wide),
        compiler_params=pltpu.CompilerParams(vmem_limit_bytes=32 * 2**20),
        cost_estimate=pl.CostEstimate(
            flops=0, transcendentals=0, bytes_accessed=6 * ranks * rows * units
        ),
    )(pieces)


class Slice:
    def __init__(self):
        self.dp = lax.axis_size("dp")
        self.context = lax.axis_size("context")
        self.ranks = self.context // 2
        self.chips = self.dp * self.context
        self.core = lax.axis_index("tensor")
        self.place = lax.axis_index("context")
        self.rank = self.place // 2
        self.side = self.place % 2
        self.line = lax.axis_index("dp")

    def send(self, block, where):
        pairs = []
        for dp in range(self.dp):
            for rank in range(self.ranks):
                for side in range(2):
                    pairs.append(
                        (self.index(dp, rank, side), self.index(*where(dp, rank, side)))
                    )
        return lax.ppermute(block, chip_axes, pairs)

    def index(self, dp, rank, side):
        return (dp * self.ranks + rank % self.ranks) * 2 + side

    def across(self, block):
        return self.send(block, lambda dp, rank, side: (dp, rank, 1 - side))

    def over(self, block):
        return self.send(block, lambda dp, rank, side: (1 - dp, rank, side))

    def along(self, block, step):
        if step % self.ranks == 0:
            return block
        return self.send(block, lambda dp, rank, side: (dp, rank + step, side))

    def swap(self, block):
        return lax.ppermute(block, "tensor", [(0, 1), (1, 0)])

    def ordered(self, mine, other):
        first = self.core == 0
        return jnp.where(first, mine, other), jnp.where(first, other, mine)

    def moves(self, block):
        return [self.along(block, step) for step in range(self.ranks)]

    def returned(self, blocks):
        total = 0.0
        for step, block in zip(range(0, self.ranks, self.ranks // len(blocks)), blocks, strict=True):
            if step:
                block = self.along(block.astype(low), -step)
            total = total + block.astype(wide)
        return total

    def to_ranks(self, array):
        pieces = [self.along(pick(array, (self.rank - step) % self.ranks, 0), -step) for step in range(self.ranks)]
        return jnp.stack(pieces)

    def exchanged(self, array):
        groups = [[rank * 2 + side for rank in range(self.ranks)] for side in range(2)]
        return lax.all_to_all(array, "context", 0, 0, tiled=True, axis_index_groups=groups)

    def turned(self, array, first):
        return lax.dynamic_slice_in_dim(jnp.concatenate([array, array]), first, array.shape[0], 0)

    def square(self):
        return [
            [self.index(dp, rank, side ^ dp) for dp in range(self.dp) for side in range(2)]
            for rank in range(self.ranks)
        ]

    def square_cores(self):
        return [[2 * chip + core for chip in chips for core in range(2)] for chips in self.square()]

    def heads_in(self, array):
        whole = lax.all_gather(
            array, all_axes, axis=0, tiled=False, axis_index_groups=self.square_cores()
        )
        return whole.reshape((4, 2) + array.shape)

    def heads_by_square(self, grads, rows):
        lanes = grads[0].shape[1]
        parts = [g.astype(low).reshape(self.dp, self.ranks, 2, rows, lanes) for g in grads]
        parts = [self.round_square(part) for part in parts]
        return jnp.stack(parts, axis=1).reshape(-1, lanes)

    def round_square(self, parts):
        return jnp.stack([parts[line, :, side ^ line] for line in range(2) for side in range(2)])

    def head_grads_out(self, parts, rows):
        total = lax.psum_scatter(
            parts,
            all_axes,
            scatter_dimension=0,
            tiled=True,
            axis_index_groups=self.square_cores(),
        )
        return total.reshape(self.ranks, rows, -1)

    def weights_in(self, array):
        ranks, rows, units = array.shape
        return lax.all_gather(array, chip_axes, axis=0, tiled=False, axis_index_groups=self.square())

    def by_model_row(self, whole):
        ranks = whole.shape[1]
        whole = self.turned(jnp.moveaxis(whole, 1, 0), ranks - self.rank)
        whole = jnp.stack(
            [whole[:, line * 2 + (side ^ line)] for line in range(2) for side in range(2)]
        ).reshape((2, 2, ranks) + whole.shape[2:])
        return jnp.transpose(whole, (0, 2, 1, 3, 4)).reshape(-1, whole.shape[-1])

    def by_square(self, grad, rows):
        parts = grad.astype(low).reshape(self.dp, self.ranks, 2, rows, -1)
        return self.round_square(parts).reshape(-1, grad.shape[1])

    def grads_out(self, parts, rows):
        total = lax.psum_scatter(
            parts, chip_axes, scatter_dimension=0, tiled=True, axis_index_groups=self.square()
        )
        return total.reshape(self.ranks, rows, -1)


def body(
    tokens,
    w_query,
    w_key,
    w_value,
    w_out,
    w_gate,
    w_up,
    w_down,
    gain_attn_in,
    gain_attn_out,
    gain_ffw_in,
    gain_ffw_out,
    cotangent,
):
    net = Slice()
    core, chips, ranks = net.core, net.chips, net.ranks
    span = tokens.shape[1]
    width = tokens.shape[2]
    half = span // 2
    rows = w_query.shape[0]
    heads = 2 * w_query.shape[1] // HEAD_DIM
    kv_heads = 2 * w_key.shape[1] // HEAD_DIM
    repeat = heads // kv_heads
    share = ranks // kv_heads
    score_scale = HEAD_DIM ** (-0.5)
    units = w_gate.shape[1] // ranks
    q_cols, k_cols = w_query.shape[1], w_key.shape[1]
    is_front = core == 0

    own_tokens = lax.dynamic_slice_in_dim(tokens[0], core * half, half, 0)
    upstream = lax.dynamic_slice_in_dim(cotangent[0], core * half, half, 0)

    front = jnp.concatenate([w_query, w_key], axis=1)
    back = jnp.concatenate([w_out, w_value], axis=1)
    mine = jnp.where(is_front, front, back)
    theirs = net.swap(jnp.where(is_front, back, front))
    low_heads, high_heads = net.ordered(mine, theirs)

    def by_group(begin, end):
        both = jnp.concatenate([low_heads[:, begin:end], high_heads[:, begin:end]], axis=1)
        return jnp.transpose(both.reshape(rows, kv_heads, -1), (1, 0, 2))

    lanes = (repeat + 1) * HEAD_DIM
    gain_row = jnp.concatenate([gain_attn_in, gain_attn_out, gain_ffw_in, gain_ffw_out])
    gain_row = jnp.pad(gain_row, (0, lanes - 4 * rows))
    head_sets = jnp.concatenate([by_group(0, q_cols), by_group(q_cols, q_cols + k_cols)], axis=2)
    head_sets = jnp.concatenate(
        [head_sets, jnp.broadcast_to(gain_row, (kv_heads, 1, lanes))], axis=1
    )
    head_sets, w_gate, w_up, w_down = hold(head_sets, w_gate, w_up, w_down)
    part = net.to_ranks(jnp.repeat(head_sets, share, axis=0))

    def by_rank(w):
        return jnp.transpose(w.reshape(rows, ranks, units), (1, 0, 2))

    gate_set, up_set, down_set = by_rank(w_gate), by_rank(w_up), by_rank(w_down)
    token_blocks = jnp.stack(net.moves(own_tokens))

    own_inputs = own_tokens.astype(wide)
    block_places = (net.rank - jnp.arange(ranks)) % ranks * 2 * span
    offsets = jnp.arange(half, dtype=jnp.int32)
    line_places = (block_places[:, None] + offsets[None, :]).reshape(-1)
    places = line_places + net.side * span + core * half
    key_places = jnp.concatenate(
        [
            line_places + side * span + of * half
            for of in (core, 1 - core)
            for side in (net.side, 1 - net.side)
        ]
    )
    exponent = jnp.arange(HEAD_DIM // 2, dtype=wide) * (-2.0 / HEAD_DIM)
    angles = places.astype(wide)[:, None] * (theta**exponent)[None, :]
    cosine, sine_part = jnp.cos(angles), jnp.sin(angles)

    by_parts = rows % 16 == 0 and units % LANES == 0
    place = jnp.stack([net.line, net.side, net.rank]).astype(jnp.int32)
    if by_parts:
        part, token_blocks, gate_set, up_set, down_set, cosine, sine_part = hold(
            part, token_blocks, gate_set, up_set, down_set, cosine, sine_part
        )
        own_units = jnp.stack([pick(w, net.rank, 0) for w in (gate_set, up_set, down_set)])
        middle_lane = (units // LANES + 1) // 2 * LANES
        upper, lower = own_units[:, :, :middle_lane], own_units[:, :, middle_lane:]
        upper = jnp.stack([upper, net.across(upper)])
        lower = jnp.stack([lower, net.over(lower)])
    else:
        part, token_blocks, gate_set, up_set, down_set = hold(
            part, token_blocks, gate_set, up_set, down_set
        )
    kept = 1 if by_parts else 0
    head_all = net.heads_in(part)
    gate_set = net.to_ranks(gate_set)
    gate_units = net.weights_in(gate_set[kept:])
    gate_set, up_set = hold(gate_set, up_set)
    up_set = net.to_ranks(up_set)
    up_units = net.weights_in(up_set[kept:])
    if by_parts:
        up_set, down_set, upper, lower = hold(up_set, down_set, upper, lower)
        upper = jnp.concatenate([upper, net.over(upper)])
        lower_side = net.across(lower)
        lower = jnp.stack([lower[0], lower_side[0], lower[1], lower_side[1]])
    else:
        up_set, down_set = hold(up_set, down_set)
    down_set = net.to_ranks(down_set)
    down_units = net.weights_in(down_set[kept:])

    asked = tuple(range(0, ranks, share))

    def asked_rows(array):
        if share == 1:
            return array
        blocks = array.reshape((ranks, half) + array.shape[1:])
        return jnp.concatenate([blocks[step] for step in asked])

    def by_head(array):
        return jnp.concatenate(jnp.split(array, repeat, axis=1))

    def by_token(array):
        return jnp.concatenate(jnp.split(array, repeat), axis=1)

    cosine_heads = jnp.concatenate([asked_rows(cosine)] * repeat)
    sine_heads = jnp.concatenate([asked_rows(sine_part)] * repeat)
    head_cols = repeat * HEAD_DIM

    def attend(head_all, token_blocks):
        if by_parts:
            front_weights, back_weights, gain_rows = by_part(place, head_all, rows)
        else:
            front_weights, back_weights = [
                net.by_model_row(head_all[:, of, :, :rows]) for of in range(2)
            ]
            gain_rows = net.by_model_row(head_all[:, 0, :, rows:])
        gains = gain_rows.reshape(chips, lanes)[:, : 4 * rows].reshape(chips, 4, rows)
        gains = jnp.transpose(gains, (1, 0, 2)).reshape(4, width).astype(wide)
        inputs = token_blocks.reshape(-1, width).astype(wide)
        normed_low = (inputs * inverse_size(inputs) * gains[0]).astype(low)
        keys = turn(product(normed_low, front_weights[:, head_cols:]), cosine, sine_part).astype(low)
        values = product(normed_low, back_weights[:, head_cols:]).astype(low)
        own_kv = jnp.concatenate([keys, values], axis=1)
        side_kv = jnp.concatenate([own_kv, net.across(own_kv)])
        all_kv = jnp.concatenate([side_kv, net.swap(side_kv)])
        queries = product(asked_rows(normed_low), front_weights[:, :head_cols])
        queries = turn(by_head(queries), cosine_heads, sine_heads).astype(low)
        allowed = key_places[None, :] <= jnp.concatenate([asked_rows(places)] * repeat)[:, None]
        scores = product_right_t(queries, all_kv[:, :HEAD_DIM]) * score_scale
        bent = jnp.tanh(scores / softcap)
        capped = jnp.where(allowed, softcap * bent, floor_value)
        shifted = jnp.exp(capped - jnp.max(capped, axis=-1, keepdims=True))
        probabilities = shifted / jnp.sum(shifted, axis=-1, keepdims=True)
        mixed = product(probabilities.astype(low), all_kv[:, HEAD_DIM:])
        mixed_low = by_token(mixed.astype(low))
        out_parts = product_right_t(mixed_low, back_weights[:, :head_cols]).astype(low)
        return (
            front_weights,
            back_weights,
            gains,
            normed_low,
            queries,
            all_kv,
            probabilities,
            bent,
            mixed_low,
            out_parts,
        )

    (
        front_weights,
        back_weights,
        gains,
        normed_low,
        queries,
        all_kv,
        probabilities,
        bent,
        mixed_low,
        out_parts,
    ) = attend(head_all, token_blocks)
    scale_in, scale_mid, scale_pre, scale_out = gains[0], gains[1], gains[2], gains[3]
    w_out_head = back_weights[:, :head_cols]
    w_value_head = back_weights[:, head_cols:]
    all_keys, all_values = all_kv[:, :HEAD_DIM], all_kv[:, HEAD_DIM:]
    probabilities_low = probabilities.astype(low)
    inputs = token_blocks.reshape(-1, width).astype(wide)
    units_in = inputs * inverse_size(inputs)
    out_parts = out_parts.reshape(len(asked), half, width).astype(wide)
    projected = 0.0
    for at, step in enumerate(asked):
        block = out_parts[at]
        if step:
            block = net.along(block.astype(low), -step).astype(wide)
        projected = projected + block


    inverse_mid = inverse_size(projected)
    unit_mid = projected * inverse_mid
    middle = own_inputs + unit_mid * scale_mid
    inverse_pre = inverse_size(middle)
    unit_pre = middle * inverse_pre
    normed_two_low = (unit_pre * scale_pre).astype(low)
    two_blocks = jnp.stack(net.moves(normed_two_low)).reshape(-1, width)
    two_blocks, gate_units, up_units = hold(two_blocks, gate_units, up_units)
    if by_parts:
        pair_units = assembled(
            place, ranks, rows, upper[:, :2], lower[:, :2], [gate_units, up_units]
        )
    else:
        pair_units = jnp.concatenate(
            [net.by_model_row(gate_units), net.by_model_row(up_units)], axis=1
        )

    all_two = jnp.concatenate([two_blocks, net.swap(two_blocks)])
    pair = product(all_two, pair_units)
    gate_in, upward = pair[:, :units], pair[:, units:]
    hidden_low = geglu(gate_in, upward).astype(low)
    hidden_low, down_units = hold(hidden_low, down_units)
    if by_parts:
        down_units = assembled(place, ranks, rows, upper[:, 2:], lower[:, 2:], [down_units])
    else:
        down_units = net.by_model_row(down_units)

    def core_total(part):
        count = ranks * half
        part = part.astype(low)
        return part[:count].astype(wide) + net.swap(part[count:]).astype(wide)

    def line_total(own):
        return net.returned(list(own.reshape(ranks, half, width)))

    branch = line_total(core_total(product_right_t(hidden_low, down_units)))
    inverse_out = inverse_size(branch)
    unit_out = branch * inverse_out
    own_output = (middle + unit_out * scale_out).astype(low)

    grad_ffw_out = jnp.sum(upstream * unit_out, axis=0)
    d_branch_low = norm_back(unit_out, inverse_out, scale_out, upstream).astype(low)
    branch_blocks = jnp.stack(net.moves(d_branch_low)).reshape(-1, width)
    all_branch = jnp.concatenate([branch_blocks, net.swap(branch_blocks)])

    down_grad = net.by_square(product_left_t(all_branch, hidden_low), rows)
    down_grad, all_branch = hold(down_grad, all_branch)
    down_grad = net.grads_out(down_grad, rows)
    d_hidden = product(all_branch, down_units)
    _, pull = jax.vjp(geglu, gate_in, upward)
    d_gate, d_up = pull(d_hidden)
    d_gate_low, d_up_low = d_gate.astype(low), d_up.astype(low)
    d_two = product_right_t(jnp.concatenate([d_gate_low, d_up_low], axis=1), pair_units)
    d_two, d_gate_low, d_up_low, all_two = hold(
        core_total(d_two), d_gate_low, d_up_low, all_two
    )
    d_normed_two = line_total(d_two)
    gate_grad = net.by_square(product_left_t(all_two, d_gate_low), rows)
    up_grad = net.by_square(product_left_t(all_two, d_up_low), rows)
    d_normed_two, gate_grad, up_grad, down_grad = hold(
        d_normed_two, gate_grad, up_grad, down_grad
    )
    gate_grad = net.grads_out(gate_grad, rows)
    grad_ffw_in = jnp.sum(d_normed_two * unit_pre, axis=0)
    d_middle = upstream + norm_back(unit_pre, inverse_pre, scale_pre, d_normed_two)
    grad_attn_out = jnp.sum(d_middle * unit_mid, axis=0)
    d_projected_low = norm_back(unit_mid, inverse_mid, scale_mid, d_middle).astype(low)
    d_projected_low, up_grad = hold(d_projected_low, up_grad)
    up_grad = net.grads_out(up_grad, rows)
    d_projected_all = jnp.stack(net.moves(d_projected_low))
    d_projected_all, down_grad = hold(d_projected_all, down_grad)
    down_grad = net.exchanged(down_grad)
    d_projected_asked = asked_rows(d_projected_all.reshape(-1, width))
    d_mixed_low = by_head(product(d_projected_asked, w_out_head).astype(low))
    d_prob = product_right_t(d_mixed_low, all_values)
    delta = jnp.sum(probabilities * d_prob, axis=-1, keepdims=True)
    d_capped = probabilities * (d_prob - delta)
    d_scores = (d_capped * (1.0 - bent * bent)).astype(low)
    d_queries = product(d_scores, all_keys) * score_scale
    d_keys = product_left_t(d_scores, queries) * score_scale
    d_values = product_left_t(probabilities_low, d_mixed_low)
    count = all_keys.shape[0] // 2
    given = jnp.concatenate([d_keys[count:].astype(low), d_values[count:].astype(low)], axis=1)
    given = net.swap(given).astype(wide)
    d_keys = d_keys[:count] + given[:, :HEAD_DIM]
    d_values = d_values[:count] + given[:, HEAD_DIM:]
    count = count // 2
    given = jnp.concatenate([d_keys[count:].astype(low), d_values[count:].astype(low)], axis=1)
    given = net.across(given).astype(wide)
    d_keys = d_keys[:count] + given[:, :HEAD_DIM]
    d_values = d_values[:count] + given[:, HEAD_DIM:]
    d_query_low = by_token(turn(d_queries, cosine_heads, -sine_heads).astype(low))
    d_key_low = turn(d_keys, cosine, -sine_part).astype(low)
    if share != 1:
        blocks = jnp.zeros((ranks, half, repeat * HEAD_DIM), low)
        d_query_low = blocks.at[jnp.array(asked)].set(
            d_query_low.reshape(len(asked), half, repeat * HEAD_DIM)
        )
        d_query_low = d_query_low.reshape(-1, repeat * HEAD_DIM)
    d_value_low = d_values.astype(low)
    d_front_low = jnp.concatenate([d_query_low, d_key_low], axis=1)
    d_normed_part = product_right_t(d_front_low, front_weights)
    d_normed_part = d_normed_part + product_right_t(d_value_low, w_value_head)
    grad_attn_in = jnp.sum(d_normed_part * units_in, axis=0)
    d_normed_low = d_normed_part.astype(low).reshape(ranks, half, width)
    d_normed_low, d_front_low, d_value_low, down_grad, gate_grad = hold(
        d_normed_low, d_front_low, d_value_low, down_grad, gate_grad
    )
    gate_grad = net.exchanged(gate_grad)
    d_normed = net.returned(list(d_normed_low))
    front_grads = product_left_t(normed_low, d_front_low)
    back_grads = jnp.concatenate(
        [
            product_left_t(d_projected_asked, mixed_low),
            product_left_t(normed_low, d_value_low),
        ],
        axis=1,
    )
    head_grads = net.heads_by_square([front_grads, back_grads], rows)
    head_grads, gate_grad = hold(head_grads, gate_grad)
    head_grads = net.head_grads_out(head_grads, rows)
    up_grad, gate_grad = hold(up_grad, gate_grad)
    up_grad = net.exchanged(up_grad)
    up_grad, head_grads = hold(up_grad, head_grads)
    gain_grads = jnp.stack([grad_attn_in, grad_attn_out, grad_ffw_in, grad_ffw_out])
    gain_grads = gain_grads + net.swap(gain_grads)
    gain_grads = jnp.transpose(gain_grads.reshape(4, net.dp, ranks, 2, rows), (1, 2, 3, 0, 4))
    gain_grads = pick(gain_grads, net.line, 0) + net.over(pick(gain_grads, 1 - net.line, 0))
    gain_grads = pick(gain_grads, net.side, 1) + net.across(pick(gain_grads, 1 - net.side, 1))
    gain_got = pick(gain_grads, net.rank, 0)
    for step in range(1, ranks):
        gain_got = gain_got + net.along(pick(gain_grads, (net.rank + step) % ranks, 0), step)
    own_inverse = inverse_size(own_inputs)
    own_grad = d_middle + norm_back(own_inputs * own_inverse, own_inverse, scale_in, d_normed)
    layer_output = jnp.concatenate(net.ordered(own_output, net.swap(own_output)))
    input_grad = jnp.concatenate(net.ordered(own_grad, net.swap(own_grad)))
    got = net.exchanged(head_grads)
    got = got.astype(wide).reshape(kv_heads, share, rows, lanes).sum(axis=1)
    got = jnp.transpose(got, (1, 0, 2)).reshape(rows, 2, kv_heads // 2, lanes)
    cut = repeat * HEAD_DIM
    total = jnp.concatenate(
        [got[..., :cut].reshape(rows, 2, -1), got[..., cut:].reshape(rows, 2, -1)], axis=2
    )
    kept = pick(total, core, 1)
    given = pick(total, 1 - core, 1)
    front, back = net.ordered(kept, net.swap(given.astype(low)).astype(wide))
    grad_query, grad_key = front[:, :q_cols], front[:, q_cols:]
    grad_out, grad_value = back[:, :q_cols], back[:, q_cols:]

    def by_units(pieces):
        if by_parts:
            return side_by_side(pieces)
        return jnp.transpose(pieces, (1, 0, 2)).reshape(rows, ranks * units).astype(wide)

    return (
        layer_output[None],
        input_grad[None],
        grad_query,
        grad_key,
        grad_value,
        grad_out,
        by_units(gate_grad),
        by_units(up_grad),
        by_units(down_grad),
        gain_got[0],
        gain_got[1],
        gain_got[2],
        gain_got[3],
    )


def solution(mesh):
    tokens_spec = P("dp", "context", None)
    weight_spec = P(("dp", "context"), "tensor")
    gain_spec = P(("dp", "context"))
    return jax.shard_map(
        body,
        mesh=mesh,
        in_specs=(tokens_spec,) + (weight_spec,) * 7 + (gain_spec,) * 4 + (tokens_spec,),
        out_specs=(tokens_spec,) * 2 + (weight_spec,) * 7 + (gain_spec,) * 4,
        check_vma=False,
    )
```

```python
import jax
import jax.numpy as jnp
from jax import lax
from jax.experimental import pallas as pl
from jax.experimental.pallas import tpu as pltpu
from jax.sharding import PartitionSpec as P

HEAD_DIM = 256
LANES = 128
LANES = 128

epsilon = 1e-06
softcap = 50.0
theta = 10000.0
floor_value = -1e30
low = jnp.bfloat16
wide = jnp.float32
chip_axes = ("dp", "context")
all_axes = ("dp", "context", "tensor")


def product(left_side, right_side):
    return jnp.dot(left_side, right_side, preferred_element_type=wide)


def product_right_t(left_side, right_side):
    return lax.dot_general(left_side, right_side, (((1,), (1,)), ((), ())), preferred_element_type=wide)


def product_left_t(left_side, right_side):
    return lax.dot_general(left_side, right_side, (((0,), (0,)), ((), ())), preferred_element_type=wide)


def inverse_size(values):
    return lax.rsqrt(jnp.mean(values * values, axis=-1, keepdims=True) + epsilon)


def norm_back(unit, inverse, scaling, upstream):
    inner = upstream * scaling
    return inverse * (inner - unit * jnp.mean(inner * unit, axis=-1, keepdims=True))


def turn(values, cosine, sine_part):
    half_width = values.shape[-1] // 2
    former = values[..., :half_width]
    latter = values[..., half_width:]
    return jnp.concatenate(
        [former * cosine - latter * sine_part, latter * cosine + former * sine_part], axis=-1
    )


def geglu(gate_in, upward):
    return jax.nn.gelu(gate_in, approximate=True) * upward


def pick(array, at, axis):
    return lax.dynamic_index_in_dim(array, at, axis, keepdims=False)


def hold(*trees):
    return lax.optimization_barrier(trees)


def assembled(place, ranks, rows, upper, lower, others):
    count, units = len(others), others[0].shape[3]
    parts = upper.shape[3], lower.shape[3]

    def kernel(place_ref, upper_ref, lower_ref, *refs):
        out, own = refs[-1], place_ref[2]
        for at in range(count):
            begin = at * units
            out[0, own, 0, :, begin : begin + parts[0]] = upper_ref[0, at]
            out[0, own, 0, :, begin + parts[0] : begin + units] = lower_ref[0, at]
            for step in range(1, ranks):
                out[0, (own + step) % ranks, 0, :, begin : begin + units] = refs[at][0, step - 1]

    def around(line, side, place):
        return (line * 2 + (side ^ line), 0, 0, 0)

    def relative(line, side, place):
        return ((line ^ place[0]) * 2 + (side ^ place[1]), 0, 0, 0)

    whole = pl.pallas_call(
        kernel,
        grid_spec=pltpu.PrefetchScalarGridSpec(
            num_scalar_prefetch=1,
            grid=(2, 2),
            in_specs=[
                pl.BlockSpec((1, count, rows, parts[0]), relative),
                pl.BlockSpec((1, count, rows, parts[1]), relative),
            ]
            + [pl.BlockSpec((1, ranks - 1, rows, units), around)] * count,
            out_specs=pl.BlockSpec(
                (1, ranks, 1, rows, count * units), lambda line, side, place: (line, 0, side, 0, 0)
            ),
        ),
        out_shape=jax.ShapeDtypeStruct((2, ranks, 2, rows, count * units), low),
        compiler_params=pltpu.CompilerParams(vmem_limit_bytes=32 * 2**20),
        cost_estimate=pl.CostEstimate(
            flops=0, transcendentals=0, bytes_accessed=16 * ranks * rows * count * units
        ),
    )(place, upper, lower, *others)
    return whole.reshape(-1, count * units)


def by_part(place, whole, rows):
    ranks, some, lanes = whole.shape[2], whole.shape[3], whole.shape[4]

    def kernel(place_ref, whole_ref, *outs):
        for core in range(2):
            for step in range(ranks):
                outs[core][0, (place_ref[2] + step) % ranks, 0] = whole_ref[0, core, step, :rows]
        for step in range(ranks):
            outs[2][0, (place_ref[2] + step) % ranks, 0] = whole_ref[0, 0, step, rows:]

    def to(count):
        return pl.BlockSpec(
            (1, ranks, 1, count, lanes), lambda line, side, place: (line, 0, side, 0, 0)
        )

    front, back, after = pl.pallas_call(
        kernel,
        grid_spec=pltpu.PrefetchScalarGridSpec(
            num_scalar_prefetch=1,
            grid=(2, 2),
            in_specs=[
                pl.BlockSpec(
                    (1,) + whole.shape[1:],
                    lambda line, side, place: (line * 2 + (side ^ line), 0, 0, 0, 0),
                )
            ],
            out_specs=[to(rows), to(rows), to(some - rows)],
        ),
        out_shape=[
            jax.ShapeDtypeStruct((2, ranks, 2, count, lanes), low)
            for count in (rows, rows, some - rows)
        ],
        compiler_params=pltpu.CompilerParams(vmem_limit_bytes=32 * 2**20),
        cost_estimate=pl.CostEstimate(
            flops=0, transcendentals=0, bytes_accessed=32 * ranks * rows * lanes
        ),
    )(place, whole)
    return front.reshape(-1, lanes), back.reshape(-1, lanes), after


def side_by_side(pieces):
    ranks, rows, units = pieces.shape

    def kernel(in_ref, out):
        for rank in range(ranks):
            out[:, rank * units : (rank + 1) * units] = in_ref[rank].astype(wide)

    return pl.pallas_call(
        kernel,
        in_specs=[pl.BlockSpec(memory_space=pltpu.VMEM)],
        out_specs=pl.BlockSpec(memory_space=pltpu.VMEM),
        out_shape=jax.ShapeDtypeStruct((rows, ranks * units), wide),
        compiler_params=pltpu.CompilerParams(vmem_limit_bytes=32 * 2**20),
        cost_estimate=pl.CostEstimate(
            flops=0, transcendentals=0, bytes_accessed=6 * ranks * rows * units
        ),
    )(pieces)


class Slice:
    def __init__(self):
        self.dp = lax.axis_size("dp")
        self.context = lax.axis_size("context")
        self.ranks = self.context // 2
        self.chips = self.dp * self.context
        self.core = lax.axis_index("tensor")
        self.place = lax.axis_index("context")
        self.rank = self.place // 2
        self.side = self.place % 2
        self.line = lax.axis_index("dp")

    def send(self, block, where):
        pairs = []
        for dp in range(self.dp):
            for rank in range(self.ranks):
                for side in range(2):
                    pairs.append(
                        (self.index(dp, rank, side), self.index(*where(dp, rank, side)))
                    )
        return lax.ppermute(block, chip_axes, pairs)

    def index(self, dp, rank, side):
        return (dp * self.ranks + rank % self.ranks) * 2 + side

    def across(self, block):
        return self.send(block, lambda dp, rank, side: (dp, rank, 1 - side))

    def over(self, block):
        return self.send(block, lambda dp, rank, side: (1 - dp, rank, side))

    def along(self, block, step):
        if step % self.ranks == 0:
            return block
        return self.send(block, lambda dp, rank, side: (dp, rank + step, side))

    def swap(self, block):
        return lax.ppermute(block, "tensor", [(0, 1), (1, 0)])

    def ordered(self, mine, other):
        first = self.core == 0
        return jnp.where(first, mine, other), jnp.where(first, other, mine)

    def moves(self, block):
        return [self.along(block, step) for step in range(self.ranks)]

    def returned(self, blocks):
        total = 0.0
        for step, block in zip(range(0, self.ranks, self.ranks // len(blocks)), blocks, strict=True):
            if step:
                block = self.along(block.astype(low), -step)
            total = total + block.astype(wide)
        return total

    def to_ranks(self, array):
        pieces = [self.along(pick(array, (self.rank - step) % self.ranks, 0), -step) for step in range(self.ranks)]
        return jnp.stack(pieces)

    def exchanged(self, array):
        groups = [[rank * 2 + side for rank in range(self.ranks)] for side in range(2)]
        return lax.all_to_all(array, "context", 0, 0, tiled=True, axis_index_groups=groups)

    def turned(self, array, first):
        return lax.dynamic_slice_in_dim(jnp.concatenate([array, array]), first, array.shape[0], 0)

    def square(self):
        return [
            [self.index(dp, rank, side ^ dp) for dp in range(self.dp) for side in range(2)]
            for rank in range(self.ranks)
        ]

    def square_cores(self):
        return [[2 * chip + core for chip in chips for core in range(2)] for chips in self.square()]

    def heads_in(self, array):
        whole = lax.all_gather(
            array, all_axes, axis=0, tiled=False, axis_index_groups=self.square_cores()
        )
        return whole.reshape((4, 2) + array.shape)

    def heads_by_square(self, grads, rows):
        lanes = grads[0].shape[1]
        parts = [g.astype(low).reshape(self.dp, self.ranks, 2, rows, lanes) for g in grads]
        parts = [self.round_square(part) for part in parts]
        return jnp.stack(parts, axis=1).reshape(-1, lanes)

    def round_square(self, parts):
        return jnp.stack([parts[line, :, side ^ line] for line in range(2) for side in range(2)])

    def head_grads_out(self, parts, rows):
        total = lax.psum_scatter(
            parts,
            all_axes,
            scatter_dimension=0,
            tiled=True,
            axis_index_groups=self.square_cores(),
        )
        return total.reshape(self.ranks, rows, -1)

    def weights_in(self, array):
        ranks, rows, units = array.shape
        return lax.all_gather(array, chip_axes, axis=0, tiled=False, axis_index_groups=self.square())

    def by_model_row(self, whole):
        ranks = whole.shape[1]
        whole = self.turned(jnp.moveaxis(whole, 1, 0), ranks - self.rank)
        whole = jnp.stack(
            [whole[:, line * 2 + (side ^ line)] for line in range(2) for side in range(2)]
        ).reshape((2, 2, ranks) + whole.shape[2:])
        return jnp.transpose(whole, (0, 2, 1, 3, 4)).reshape(-1, whole.shape[-1])

    def by_square(self, grad, rows):
        parts = grad.astype(low).reshape(self.dp, self.ranks, 2, rows, -1)
        return self.round_square(parts).reshape(-1, grad.shape[1])

    def grads_out(self, parts, rows):
        total = lax.psum_scatter(
            parts, chip_axes, scatter_dimension=0, tiled=True, axis_index_groups=self.square()
        )
        return total.reshape(self.ranks, rows, -1)


def body(
    tokens,
    w_query,
    w_key,
    w_value,
    w_out,
    w_gate,
    w_up,
    w_down,
    gain_attn_in,
    gain_attn_out,
    gain_ffw_in,
    gain_ffw_out,
    cotangent,
):
    net = Slice()
    core, chips, ranks = net.core, net.chips, net.ranks
    span = tokens.shape[1]
    width = tokens.shape[2]
    half = span // 2
    rows = w_query.shape[0]
    heads = 2 * w_query.shape[1] // HEAD_DIM
    kv_heads = 2 * w_key.shape[1] // HEAD_DIM
    repeat = heads // kv_heads
    share = ranks // kv_heads
    score_scale = HEAD_DIM ** (-0.5)
    units = w_gate.shape[1] // ranks
    q_cols, k_cols = w_query.shape[1], w_key.shape[1]
    is_front = core == 0

    own_tokens = lax.dynamic_slice_in_dim(tokens[0], core * half, half, 0)
    upstream = lax.dynamic_slice_in_dim(cotangent[0], core * half, half, 0)

    front = jnp.concatenate([w_query, w_key], axis=1)
    back = jnp.concatenate([w_out, w_value], axis=1)
    mine = jnp.where(is_front, front, back)
    theirs = net.swap(jnp.where(is_front, back, front))
    low_heads, high_heads = net.ordered(mine, theirs)

    def by_group(begin, end):
        both = jnp.concatenate([low_heads[:, begin:end], high_heads[:, begin:end]], axis=1)
        return jnp.transpose(both.reshape(rows, kv_heads, -1), (1, 0, 2))

    lanes = (repeat + 1) * HEAD_DIM
    gain_row = jnp.concatenate([gain_attn_in, gain_attn_out, gain_ffw_in, gain_ffw_out])
    gain_row = jnp.pad(gain_row, (0, lanes - 4 * rows))
    head_sets = jnp.concatenate([by_group(0, q_cols), by_group(q_cols, q_cols + k_cols)], axis=2)
    head_sets = jnp.concatenate(
        [head_sets, jnp.broadcast_to(gain_row, (kv_heads, 1, lanes))], axis=1
    )
    head_sets, w_gate, w_up, w_down = hold(head_sets, w_gate, w_up, w_down)
    part = net.to_ranks(jnp.repeat(head_sets, share, axis=0))

    def by_rank(w):
        return jnp.transpose(w.reshape(rows, ranks, units), (1, 0, 2))

    gate_set, up_set, down_set = by_rank(w_gate), by_rank(w_up), by_rank(w_down)
    token_blocks = jnp.stack(net.moves(own_tokens))

    own_inputs = own_tokens.astype(wide)
    block_places = (net.rank - jnp.arange(ranks)) % ranks * 2 * span
    offsets = jnp.arange(half, dtype=jnp.int32)
    line_places = (block_places[:, None] + offsets[None, :]).reshape(-1)
    places = line_places + net.side * span + core * half
    key_places = jnp.concatenate(
        [
            line_places + side * span + of * half
            for of in (core, 1 - core)
            for side in (net.side, 1 - net.side)
        ]
    )
    exponent = jnp.arange(HEAD_DIM // 2, dtype=wide) * (-2.0 / HEAD_DIM)
    angles = places.astype(wide)[:, None] * (theta**exponent)[None, :]
    cosine, sine_part = jnp.cos(angles), jnp.sin(angles)

    by_parts = rows % 16 == 0 and units % LANES == 0
    place = jnp.stack([net.line, net.side, net.rank]).astype(jnp.int32)
    if by_parts:
        part, token_blocks, gate_set, up_set, down_set, cosine, sine_part = hold(
            part, token_blocks, gate_set, up_set, down_set, cosine, sine_part
        )
        own_units = jnp.stack([pick(w, net.rank, 0) for w in (gate_set, up_set, down_set)])
        middle_lane = (units // LANES + 1) // 2 * LANES
        upper, lower = own_units[:, :, :middle_lane], own_units[:, :, middle_lane:]
        upper = jnp.stack([upper, net.across(upper)])
        lower = jnp.stack([lower, net.over(lower)])
    else:
        part, token_blocks, gate_set, up_set, down_set = hold(
            part, token_blocks, gate_set, up_set, down_set
        )
    kept = 1 if by_parts else 0
    head_all = net.heads_in(part)
    gate_set = net.to_ranks(gate_set)
    gate_units = net.weights_in(gate_set[kept:])
    gate_set, up_set = hold(gate_set, up_set)
    up_set = net.to_ranks(up_set)
    up_units = net.weights_in(up_set[kept:])
    if by_parts:
        up_set, down_set, upper, lower = hold(up_set, down_set, upper, lower)
        upper = jnp.concatenate([upper, net.over(upper)])
        lower_side = net.across(lower)
        lower = jnp.stack([lower[0], lower_side[0], lower[1], lower_side[1]])
    else:
        up_set, down_set = hold(up_set, down_set)
    down_set = net.to_ranks(down_set)
    down_units = net.weights_in(down_set[kept:])

    asked = tuple(range(0, ranks, share))

    def asked_rows(array):
        if share == 1:
            return array
        blocks = array.reshape((ranks, half) + array.shape[1:])
        return jnp.concatenate([blocks[step] for step in asked])

    def by_head(array):
        return jnp.concatenate(jnp.split(array, repeat, axis=1))

    def by_token(array):
        return jnp.concatenate(jnp.split(array, repeat), axis=1)

    cosine_heads = jnp.concatenate([asked_rows(cosine)] * repeat)
    sine_heads = jnp.concatenate([asked_rows(sine_part)] * repeat)
    head_cols = repeat * HEAD_DIM

    def attend(head_all, token_blocks):
        if by_parts:
            front_weights, back_weights, gain_rows = by_part(place, head_all, rows)
        else:
            front_weights, back_weights = [
                net.by_model_row(head_all[:, of, :, :rows]) for of in range(2)
            ]
            gain_rows = net.by_model_row(head_all[:, 0, :, rows:])
        gains = gain_rows.reshape(chips, lanes)[:, : 4 * rows].reshape(chips, 4, rows)
        gains = jnp.transpose(gains, (1, 0, 2)).reshape(4, width).astype(wide)
        inputs = token_blocks.reshape(-1, width).astype(wide)
        normed_low = (inputs * inverse_size(inputs) * gains[0]).astype(low)
        keys = turn(product(normed_low, front_weights[:, head_cols:]), cosine, sine_part).astype(low)
        values = product(normed_low, back_weights[:, head_cols:]).astype(low)
        own_kv = jnp.concatenate([keys, values], axis=1)
        side_kv = jnp.concatenate([own_kv, net.across(own_kv)])
        all_kv = jnp.concatenate([side_kv, net.swap(side_kv)])
        queries = product(asked_rows(normed_low), front_weights[:, :head_cols])
        queries = turn(by_head(queries), cosine_heads, sine_heads).astype(low)
        allowed = key_places[None, :] <= jnp.concatenate([asked_rows(places)] * repeat)[:, None]
        scores = product_right_t(queries, all_kv[:, :HEAD_DIM]) * score_scale
        bent = jnp.tanh(scores / softcap)
        capped = jnp.where(allowed, softcap * bent, floor_value)
        shifted = jnp.exp(capped - jnp.max(capped, axis=-1, keepdims=True))
        probabilities = shifted / jnp.sum(shifted, axis=-1, keepdims=True)
        mixed = product(probabilities.astype(low), all_kv[:, HEAD_DIM:])
        mixed_low = by_token(mixed.astype(low))
        out_parts = product_right_t(mixed_low, back_weights[:, :head_cols]).astype(low)
        return (
            front_weights,
            back_weights,
            gains,
            normed_low,
            queries,
            all_kv,
            probabilities,
            bent,
            mixed_low,
            out_parts,
        )

    (
        front_weights,
        back_weights,
        gains,
        normed_low,
        queries,
        all_kv,
        probabilities,
        bent,
        mixed_low,
        out_parts,
    ) = attend(head_all, token_blocks)
    scale_in, scale_mid, scale_pre, scale_out = gains[0], gains[1], gains[2], gains[3]
    w_out_head = back_weights[:, :head_cols]
    w_value_head = back_weights[:, head_cols:]
    all_keys, all_values = all_kv[:, :HEAD_DIM], all_kv[:, HEAD_DIM:]
    probabilities_low = probabilities.astype(low)
    inputs = token_blocks.reshape(-1, width).astype(wide)
    units_in = inputs * inverse_size(inputs)
    out_parts = out_parts.reshape(len(asked), half, width).astype(wide)
    projected = 0.0
    for at, step in enumerate(asked):
        block = out_parts[at]
        if step:
            block = net.along(block.astype(low), -step).astype(wide)
        projected = projected + block


    inverse_mid = inverse_size(projected)
    unit_mid = projected * inverse_mid
    middle = own_inputs + unit_mid * scale_mid
    inverse_pre = inverse_size(middle)
    unit_pre = middle * inverse_pre
    normed_two_low = (unit_pre * scale_pre).astype(low)
    two_blocks = jnp.stack(net.moves(normed_two_low)).reshape(-1, width)
    two_blocks, gate_units, up_units = hold(two_blocks, gate_units, up_units)
    if by_parts:
        pair_units = assembled(
            place, ranks, rows, upper[:, :2], lower[:, :2], [gate_units, up_units]
        )
    else:
        pair_units = jnp.concatenate(
            [net.by_model_row(gate_units), net.by_model_row(up_units)], axis=1
        )

    all_two = jnp.concatenate([two_blocks, net.swap(two_blocks)])
    pair = product(all_two, pair_units)
    gate_in, upward = pair[:, :units], pair[:, units:]
    hidden_low = geglu(gate_in, upward).astype(low)
    hidden_low, down_units = hold(hidden_low, down_units)
    if by_parts:
        down_units = assembled(place, ranks, rows, upper[:, 2:], lower[:, 2:], [down_units])
    else:
        down_units = net.by_model_row(down_units)

    def core_total(part):
        count = ranks * half
        part = part.astype(low)
        return part[:count].astype(wide) + net.swap(part[count:]).astype(wide)

    def line_total(own):
        return net.returned(list(own.reshape(ranks, half, width)))

    branch = line_total(core_total(product_right_t(hidden_low, down_units)))
    inverse_out = inverse_size(branch)
    unit_out = branch * inverse_out
    own_output = (middle + unit_out * scale_out).astype(low)

    grad_ffw_out = jnp.sum(upstream * unit_out, axis=0)
    d_branch_low = norm_back(unit_out, inverse_out, scale_out, upstream).astype(low)
    branch_blocks = jnp.stack(net.moves(d_branch_low)).reshape(-1, width)
    all_branch = jnp.concatenate([branch_blocks, net.swap(branch_blocks)])

    down_grad = net.by_square(product_left_t(all_branch, hidden_low), rows)
    down_grad = net.grads_out(down_grad, rows)
    d_hidden = product(all_branch, down_units)
    _, pull = jax.vjp(geglu, gate_in, upward)
    d_gate, d_up = pull(d_hidden)
    d_gate_low, d_up_low = d_gate.astype(low), d_up.astype(low)
    d_two = product_right_t(jnp.concatenate([d_gate_low, d_up_low], axis=1), pair_units)
    d_two, d_gate_low, d_up_low, all_two = hold(
        core_total(d_two), d_gate_low, d_up_low, all_two
    )
    d_normed_two = line_total(d_two)
    gate_grad = net.by_square(product_left_t(all_two, d_gate_low), rows)
    up_grad = net.by_square(product_left_t(all_two, d_up_low), rows)
    d_normed_two, gate_grad, up_grad, down_grad = hold(
        d_normed_two, gate_grad, up_grad, down_grad
    )
    gate_grad = net.grads_out(gate_grad, rows)
    grad_ffw_in = jnp.sum(d_normed_two * unit_pre, axis=0)
    d_middle = upstream + norm_back(unit_pre, inverse_pre, scale_pre, d_normed_two)
    grad_attn_out = jnp.sum(d_middle * unit_mid, axis=0)
    d_projected_low = norm_back(unit_mid, inverse_mid, scale_mid, d_middle).astype(low)
    d_projected_low, up_grad = hold(d_projected_low, up_grad)
    up_grad = net.grads_out(up_grad, rows)
    d_projected_all = jnp.stack(net.moves(d_projected_low))
    d_projected_all, down_grad = hold(d_projected_all, down_grad)
    down_grad = net.exchanged(down_grad)
    d_projected_asked = asked_rows(d_projected_all.reshape(-1, width))
    d_mixed_low = by_head(product(d_projected_asked, w_out_head).astype(low))
    d_prob = product_right_t(d_mixed_low, all_values)
    delta = jnp.sum(probabilities * d_prob, axis=-1, keepdims=True)
    d_capped = probabilities * (d_prob - delta)
    d_scores = (d_capped * (1.0 - bent * bent)).astype(low)
    d_queries = product(d_scores, all_keys) * score_scale
    d_keys = product_left_t(d_scores, queries) * score_scale
    d_values = product_left_t(probabilities_low, d_mixed_low)
    count = all_keys.shape[0] // 2
    given = jnp.concatenate([d_keys[count:].astype(low), d_values[count:].astype(low)], axis=1)
    given = net.swap(given).astype(wide)
    d_keys = d_keys[:count] + given[:, :HEAD_DIM]
    d_values = d_values[:count] + given[:, HEAD_DIM:]
    count = count // 2
    given = jnp.concatenate([d_keys[count:].astype(low), d_values[count:].astype(low)], axis=1)
    given = net.across(given).astype(wide)
    d_keys = d_keys[:count] + given[:, :HEAD_DIM]
    d_values = d_values[:count] + given[:, HEAD_DIM:]
    d_query_low = by_token(turn(d_queries, cosine_heads, -sine_heads).astype(low))
    d_key_low = turn(d_keys, cosine, -sine_part).astype(low)
    if share != 1:
        blocks = jnp.zeros((ranks, half, repeat * HEAD_DIM), low)
        d_query_low = blocks.at[jnp.array(asked)].set(
            d_query_low.reshape(len(asked), half, repeat * HEAD_DIM)
        )
        d_query_low = d_query_low.reshape(-1, repeat * HEAD_DIM)
    d_value_low = d_values.astype(low)
    d_front_low = jnp.concatenate([d_query_low, d_key_low], axis=1)
    d_normed_part = product_right_t(d_front_low, front_weights)
    d_normed_part = d_normed_part + product_right_t(d_value_low, w_value_head)
    grad_attn_in = jnp.sum(d_normed_part * units_in, axis=0)
    d_normed_low = d_normed_part.astype(low).reshape(ranks, half, width)
    d_normed_low, d_front_low, d_value_low, down_grad, gate_grad = hold(
        d_normed_low, d_front_low, d_value_low, down_grad, gate_grad
    )
    gate_grad = net.exchanged(gate_grad)
    d_normed = net.returned(list(d_normed_low))
    front_grads = product_left_t(normed_low, d_front_low)
    back_grads = jnp.concatenate(
        [
            product_left_t(d_projected_asked, mixed_low),
            product_left_t(normed_low, d_value_low),
        ],
        axis=1,
    )
    head_grads = net.heads_by_square([front_grads, back_grads], rows)
    head_grads, gate_grad = hold(head_grads, gate_grad)
    head_grads = net.head_grads_out(head_grads, rows)
    up_grad, gate_grad = hold(up_grad, gate_grad)
    up_grad = net.exchanged(up_grad)
    up_grad, head_grads = hold(up_grad, head_grads)
    gain_grads = jnp.stack([grad_attn_in, grad_attn_out, grad_ffw_in, grad_ffw_out])
    gain_grads = gain_grads + net.swap(gain_grads)
    gain_grads = jnp.transpose(gain_grads.reshape(4, net.dp, ranks, 2, rows), (1, 2, 3, 0, 4))
    gain_grads = pick(gain_grads, net.line, 0) + net.over(pick(gain_grads, 1 - net.line, 0))
    gain_grads = pick(gain_grads, net.side, 1) + net.across(pick(gain_grads, 1 - net.side, 1))
    gain_got = pick(gain_grads, net.rank, 0)
    for step in range(1, ranks):
        gain_got = gain_got + net.along(pick(gain_grads, (net.rank + step) % ranks, 0), step)
    own_inverse = inverse_size(own_inputs)
    own_grad = d_middle + norm_back(own_inputs * own_inverse, own_inverse, scale_in, d_normed)
    layer_output = jnp.concatenate(net.ordered(own_output, net.swap(own_output)))
    input_grad = jnp.concatenate(net.ordered(own_grad, net.swap(own_grad)))
    got = net.exchanged(head_grads)
    got = got.astype(wide).reshape(kv_heads, share, rows, lanes).sum(axis=1)
    got = jnp.transpose(got, (1, 0, 2)).reshape(rows, 2, kv_heads // 2, lanes)
    cut = repeat * HEAD_DIM
    total = jnp.concatenate(
        [got[..., :cut].reshape(rows, 2, -1), got[..., cut:].reshape(rows, 2, -1)], axis=2
    )
    kept = pick(total, core, 1)
    given = pick(total, 1 - core, 1)
    front, back = net.ordered(kept, net.swap(given.astype(low)).astype(wide))
    grad_query, grad_key = front[:, :q_cols], front[:, q_cols:]
    grad_out, grad_value = back[:, :q_cols], back[:, q_cols:]

    def by_units(pieces):
        if by_parts:
            return side_by_side(pieces)
        return jnp.transpose(pieces, (1, 0, 2)).reshape(rows, ranks * units).astype(wide)

    return (
        layer_output[None],
        input_grad[None],
        grad_query,
        grad_key,
        grad_value,
        grad_out,
        by_units(gate_grad),
        by_units(up_grad),
        by_units(down_grad),
        gain_got[0],
        gain_got[1],
        gain_got[2],
        gain_got[3],
    )


def solution(mesh):
    tokens_spec = P("dp", "context", None)
    weight_spec = P(("dp", "context"), "tensor")
    gain_spec = P(("dp", "context"))
    return jax.shard_map(
        body,
        mesh=mesh,
        in_specs=(tokens_spec,) + (weight_spec,) * 7 + (gain_spec,) * 4 + (tokens_spec,),
        out_specs=(tokens_spec,) * 2 + (weight_spec,) * 7 + (gain_spec,) * 4,
        check_vma=False,
    )
```
